256 devices in a mesh: rep: 4 (over y), seq: 32 (over x, z), cfg: 2 (over core).
Axes of the slice: x: 4, y: 4, z: 8, core: 2. Of those that a mesh axis runs over, the one named last changes fastest.
Arguments:
- tokens: bfloat16 [128, 512, 1152], P(('rep', 'seq')), parts along dimension 0, may hold values from -36 to 36
- modulation: float32 [2, 6, 1152], P('cfg'), may hold values from -3 to 3
- w_qkv_s: bfloat16 [1152, 3456], P(None, ('seq', 'cfg')), may hold values from -0.1875 to 0.1875
- w_out_s: bfloat16 [1152, 1152], P(None, ('seq', 'cfg')), may hold values from -0.1875 to 0.1875
- w_qkv_t: bfloat16 [1152, 3456], P(None, ('seq', 'cfg')), may hold values from -0.1875 to 0.1875
- w_out_t: bfloat16 [1152, 1152], P(None, ('seq', 'cfg')), may hold values from -0.1875 to 0.1875
- w_final: bfloat16 [1152, 16], replicated, may hold values from -0.1875 to 0.1875
- norm_gains: float32 [4, 72], replicated, may hold values from 0.25 to 1.75
- clip_tokens: int32 [32], P('rep'), parts along dimension 0, may hold values from 64 to 512, as said below
- block_clip: int32 [128], P('rep'), parts along dimension 0, may hold values from 0 to 7, never falling along the last dimension, each value on 1 to 8 neighbouring positions
Outputs:
- guided: float32 [128, 512, 16], P('rep', 'seq', 'cfg'), parts along dimension 0
The draws below stay inside these ranges and needn't reach their ends.
There are 4 independent parts, one for each index of `rep`. The reference program is written for one: setup_inputs(seed, part) draws one part's arguments, and reference() takes and returns one part's arrays. A program takes and returns all parts, laid end to end along the dimension named above; an argument that names none is the same for every part. Nothing has to cross between parts.
Inputs may be any that keep to these rules, and one draw needn't show every extreme that they name: `clip_tokens`: one clip has exactly 512 spatial tokens. `block_clip`: never falling along the blocks; every clip has 1 to 8 blocks, one exactly 8.
All inputs are finite; a program needn't handle non-finite values.
Results may differ from the reference program's by a relative error of at most 0.019.
Values may be sent and summed in bfloat16 or wider, within the bound.
No kernel may reach another device: no remote copies, remote signals or barrier semaphores. Data moves between devices by JAX's collectives and lax.ppermute only.
A program may use at most 128 MiB of HBM per device.

```python
import math
import jax
import jax.numpy as jnp
import numpy as np
from jax import lax

D = 1152
HD = 72
COUT = 16
BLK = 512
FRAMES = 32
CLIPS = 8
FRAMES_MOST = 8


def draw_tokens(key, part):
    key = jax.random.fold_in(key, 5)
    base_key, row_key, column_key = jax.random.split(key, 3)
    base = jnp.clip(jax.random.normal(base_key, (FRAMES, BLK, D), jnp.float32), -4.0, 4.0)
    row_scale = jnp.exp(jax.random.uniform(row_key, (FRAMES, BLK, 1), jnp.float32, math.log(0.3), math.log(3.0)))
    column_scale = jnp.exp(jax.random.uniform(column_key, (1, 1, D), jnp.float32, math.log(0.3), math.log(3.0)))
    return (base * row_scale * column_scale).astype(jnp.bfloat16)


def draw_clip_tokens(key, part):
    key = jax.random.fold_in(key, 11)
    count_key, chosen_key = jax.random.split(key)
    counts = jax.random.randint(count_key, (CLIPS,), BLK // 8, BLK + 1)
    chosen = jax.random.randint(chosen_key, (), 0, CLIPS)
    counts = jnp.where(jnp.arange(CLIPS) == chosen, BLK, counts)
    return counts.astype(jnp.int32)


def steps_of(stream_key, shape, pieces, smallest, high):
    def one(position, parts):
        heights = jax.random.uniform(jax.random.fold_in(jax.random.fold_in(stream_key, 6), position), (parts,), jnp.float32, smallest / len(pieces), high / len(pieces))
        return jnp.repeat(jnp.exp(heights), shape[position] // parts).reshape((-1,) + (1,) * (len(shape) - position - 1))

    level = one(*pieces[0])
    for cut in pieces[1:]:
        level = level * one(*cut)
    return level


def split_up(amount, total, limit, skew):
    weights = [(1 << 20) // math.isqrt(rank ** skew) + 1 for rank in range(2, amount + 1)]
    rest, given = total - limit - (amount - 1), [1] * (amount - 1)
    while rest > 0:
        candidates = [i for i in range(amount - 1) if given[i] < limit]
        whole, left = sum([weights[i] for i in candidates]), rest
        for i in candidates:
            addition = min(limit - given[i], max(1, left * weights[i] // whole), rest)
            given[i] = given[i] + addition
            rest = rest - addition
    return np.array([limit] + given)


def ragged(rng, amount, total, reach, lean):
    if amount == 2:
        one = jax.random.randint(rng, (), max(1, total - reach), min(reach, total - 1) + 1)
        return jnp.stack([one, total - one])
    sizes = jnp.asarray(split_up(amount, total, reach, lean), jnp.int32)
    pairs = (amount - 1) // 2
    source_of, taker = sizes[1:1 + 2 * pairs:2], sizes[2:2 + 2 * pairs:2]
    room = jnp.minimum(source_of - 1, reach - taker)
    passed = jax.random.randint(jax.random.fold_in(rng, 1), (pairs,), 0, 1 << 20) % (room + 1)
    sizes = sizes.at[1:1 + 2 * pairs:2].set(source_of - passed).at[2:2 + 2 * pairs:2].set(taker + passed)
    return sizes[jax.random.permutation(jax.random.fold_in(rng, 2), amount)]


def normal_values(rng, shape, spread, limit, shards=(), kind=jnp.bfloat16):
    values = jax.random.normal(rng, shape, jnp.float32) * spread
    if len(shards) > 0:
        values = steps_of(rng, shape, shards, -0.22, 0.18) * values
    return jnp.clip(values, min=-limit, max=limit).astype(kind)


def setup_inputs(seed: int = 0, part: int = 0) -> dict:
    keys = jax.random.split(jax.random.key(seed), 11)
    own_keys = jax.random.split(jax.random.fold_in(keys[10], part), 11)
    return {
        "tokens": draw_tokens(jax.random.fold_in(jax.random.fold_in(keys[10], part), 71), part),
        "modulation": normal_values(keys[1], (2, 6, D), 0.5, 3.0, ((0, 2),), jnp.float32),
        "w_qkv_s": normal_values(keys[2], (D, 3 * D), D ** -0.5, 0.1875, ((1, 64),)),
        "w_out_s": normal_values(keys[3], (D, D), D ** -0.5, 0.1875, ((1, 64),)),
        "w_qkv_t": normal_values(keys[4], (D, 3 * D), D ** -0.5, 0.1875, ((1, 64),)),
        "w_out_t": normal_values(keys[5], (D, D), D ** -0.5, 0.1875, ((1, 64),)),
        "w_final": normal_values(keys[6], (D, COUT), D ** -0.5, 0.1875),
        "norm_gains": jnp.clip(1.0 + 0.15 * jax.random.normal(keys[7], (4, HD), jnp.float32), 0.25, 1.75),
        "clip_tokens": draw_clip_tokens(jax.random.fold_in(jax.random.fold_in(keys[10], part), 71), part),
        "block_clip": jnp.searchsorted(jnp.cumsum(ragged(own_keys[9], CLIPS, FRAMES, FRAMES_MOST, 1)), jnp.arange(FRAMES), side="right").astype(jnp.int32),
    }


def layer_norm(values_in):
    average = lax.optimization_barrier(jnp.mean(values_in, axis=-1, keepdims=True))
    centred = values_in - average
    variance = lax.optimization_barrier(jnp.mean(centred * centred, axis=-1, keepdims=True))
    return centred * lax.rsqrt(variance + 1e-06)

def modulate(values_in, scale_row, offset_row):
    return (layer_norm(values_in.astype(jnp.float32)) * (1.0 + scale_row) + offset_row).astype(jnp.bfloat16)

def head_scale(values_in, gains_row):
    return (values_in * lax.rsqrt(lax.optimization_barrier(jnp.mean(values_in * values_in, axis=-1, keepdims=True)) + 1e-06) * gains_row).astype(jnp.bfloat16)

def spatial_attend(projected, length, norm_gains):
    row_count = projected.shape[0]
    features = projected.shape[1] // 3
    head_size = norm_gains.shape[1]
    head_count = features // head_size
    queries = head_scale(projected[:, :features].reshape(row_count, head_count, head_size), norm_gains[0])
    key_rows = head_scale(projected[:, features:2 * features].reshape(row_count, head_count, head_size), norm_gains[1])
    values = projected[:, 2 * features:].reshape(row_count, head_count, head_size).astype(jnp.bfloat16)
    scores = jnp.einsum('qhd,khd->hqk', queries.astype(jnp.float32), key_rows.astype(jnp.float32)) / math.sqrt(head_size)
    allowed = (jnp.arange(row_count, dtype=jnp.int32) < length)[None, None, :]
    unnormed = jnp.where(allowed, jnp.exp(scores), 0.0)
    shares = (unnormed / lax.optimization_barrier(jnp.sum(unnormed, axis=-1, keepdims=True))).astype(jnp.bfloat16)
    attended = jnp.einsum('hqk,khd->qhd', shares.astype(jnp.float32), values.astype(jnp.float32))
    return attended.astype(jnp.bfloat16).reshape(row_count, features)

def temporal_attend(projected, same_clip, norm_gains):
    frames, locations, triple = projected.shape
    features = triple // 3
    head_size = norm_gains.shape[1]
    head_count = features // head_size
    queries = head_scale(projected[..., :features].reshape(frames, locations, head_count, head_size), norm_gains[2])
    key_rows = head_scale(projected[..., features:2 * features].reshape(frames, locations, head_count, head_size), norm_gains[3])
    values = projected[..., 2 * features:].reshape(frames, locations, head_count, head_size).astype(jnp.bfloat16)
    scores = jnp.einsum('blhd,clhd->lhbc', queries.astype(jnp.float32), key_rows.astype(jnp.float32)) / math.sqrt(head_size)
    unnormed = jnp.where(same_clip[None, None], jnp.exp(scores), 0.0)
    shares = (unnormed / lax.optimization_barrier(jnp.sum(unnormed, axis=-1, keepdims=True))).astype(jnp.bfloat16)
    attended = jnp.einsum('lhbc,clhd->blhd', shares.astype(jnp.float32), values.astype(jnp.float32))
    return attended.astype(jnp.bfloat16).reshape(frames, locations, features)

def reference(tokens, modulation, w_qkv_s, w_out_s, w_qkv_t, w_out_t, w_final, norm_gains, clip_tokens, block_clip):
    frames, block_tokens, features = tokens.shape
    lengths = clip_tokens[block_clip].astype(jnp.int32)
    inside = jnp.arange(block_tokens, dtype=jnp.int32)[None, :] < lengths[:, None]
    same_clip = block_clip[:, None] == block_clip[None, :]
    predictions = []
    for branch in range(2):
        levels = modulation[branch]

        def spatial_block(packed):
            block, length = packed
            normed = modulate(block, levels[1], levels[0])
            projected = jnp.dot(normed, w_qkv_s, preferred_element_type=jnp.float32)
            attended = spatial_attend(projected, length, norm_gains)
            projection = jnp.dot(attended, w_out_s, preferred_element_type=jnp.float32)
            return (block.astype(jnp.float32) + levels[2] * projection).astype(jnp.bfloat16)
        residual = lax.map(spatial_block, (tokens, lengths))
        temporal_in = modulate(residual, levels[4], levels[3])
        projected = jnp.dot(temporal_in.reshape(-1, features), w_qkv_t, preferred_element_type=jnp.float32)
        projected = projected.reshape(frames, block_tokens, 3 * features)
        temporal_out = temporal_attend(projected, same_clip, norm_gains)
        projection = jnp.dot(temporal_out.reshape(-1, features), w_out_t, preferred_element_type=jnp.float32)
        updated = residual.astype(jnp.float32) + levels[5] * projection.reshape(frames, block_tokens, features)
        final_in = layer_norm(updated).astype(jnp.bfloat16)
        predicted = jnp.dot(final_in.reshape(-1, features), w_final, preferred_element_type=jnp.float32)
        predictions.append(predicted.reshape(frames, block_tokens, -1))
    conditional, unconditional = (predictions[0], predictions[1])
    guided = unconditional + 7.0 * (conditional - unconditional)
    return jnp.where(inside[:, :, None], guided, 0.0)
```

```python
import functools
import math

import jax
import jax.numpy as jnp
from jax import lax
from jax.experimental import pallas as pl
from jax.experimental.pallas import tpu as pltpu
from jax.sharding import PartitionSpec as P

BF16 = jnp.bfloat16
F32 = jnp.float32
LANES = 128
TEMPORAL_ROWS = 128


def dot_nt(left, right):
    return lax.dot_general(left, right, (((1,), (1,)), ((), ())), preferred_element_type=F32)


def layer_norm(values_in):
    average = jnp.mean(values_in, axis=-1, keepdims=True)
    centred = values_in - average
    variance = jnp.mean(centred * centred, axis=-1, keepdims=True)
    return centred * lax.rsqrt(variance + 1e-06)


def modulate_rows(source, target, scale_row, offset_row, step):
    def chunk(i, carry):
        rows = pl.ds(pl.multiple_of(i * step, step), step)
        target[rows, :] = (layer_norm(source[rows, :].astype(F32)) * (1.0 + scale_row) + offset_row).astype(BF16)
        return carry

    lax.fori_loop(0, source.shape[0] // step, chunk, 0)


def lay_out_weights(landing, heads, out_rows, head_size):
    share = 3 * head_size // 4
    quarter = head_size // 4
    width = landing.shape[2]
    head_count = heads.shape[1]
    blank = jnp.zeros((LANES - head_size, width), BF16)

    def group(g, carry):
        for half in range(2):
            part = [landing[8 * g + 4 * half + i] for i in range(4)]
            pieces = (
                (part[0][:share], part[1][: head_size - share]),
                (part[1][head_size - share : share], part[2][: 2 * quarter]),
                (part[2][2 * quarter : share], part[3][:share]),
            )
            for i in range(3):
                block = 6 * g + 3 * half + i
                heads[block // head_count, block % head_count] = jnp.concatenate(pieces[i] + (blank,), axis=0)
        rows = [landing[8 * g + i][share:] for i in range(8)]
        size = 8 * quarter
        out_rows[pl.ds(pl.multiple_of(g * size, 16), size), :] = jnp.concatenate(rows, axis=0)
        return carry

    lax.fori_loop(0, landing.shape[0] // 8, group, 0)


def unit_heads(projected, gain_row, head_size, factor):
    total = jnp.sum(projected * projected, axis=-1, keepdims=True)
    return (projected * lax.rsqrt(total / head_size + 1e-06) * (gain_row * factor)).astype(BF16)


def project_pair(normed, heads, pair):
    found = []
    for kind in range(3):
        weight = heads[kind, pl.ds(2 * pair, 2)].reshape(2 * LANES, normed.shape[1])
        found.append(dot_nt(normed[...], weight))
    return found


def gather_heads(attended, packed, head_size, step):
    def chunk(i, carry):
        rows = pl.ds(pl.multiple_of(i * step, step), step)
        packed[rows, :] = jnp.concatenate(
            [attended[h, rows, :][:, :head_size] for h in range(attended.shape[0])], axis=1
        )
        return carry

    lax.fori_loop(0, packed.shape[0] // step, chunk, 0)


def spatial_kernel(head_size, length_ref, tokens, levels, gains, gathered, residual,
                   landing, heads, out_rows, normed, attended, packed, sem):
    arriving = pltpu.make_async_copy(gathered.at[:, 0], landing, sem)
    arriving.start()
    modulate_rows(tokens, normed, levels[1:2, :], levels[0:1, :], 64)
    arriving.wait()
    lay_out_weights(landing, heads, out_rows, head_size)
    row_count = tokens.shape[0]
    inside = lax.broadcasted_iota(jnp.int32, (row_count, LANES), 0) < length_ref[0]
    column = lax.broadcasted_iota(jnp.int32, (row_count, LANES), 1)
    factor = math.log2(math.e) / math.sqrt(head_size)

    def pair_step(pair, carry):
        queries, keys, values = project_pair(normed, heads, pair)
        for i in range(2):
            lanes = slice(i * LANES, (i + 1) * LANES)
            query = unit_heads(queries[:, lanes], gains[0:1, :], head_size, factor)
            key = unit_heads(keys[:, lanes], gains[1:2, :], head_size, 1.0)
            value = jnp.where(column == head_size, 1.0, values[:, lanes])
            value = jnp.where(inside, value, 0.0).astype(BF16)
            unnormed = jnp.exp2(dot_nt(query, key)).astype(BF16)
            summed = jnp.dot(unnormed, value, preferred_element_type=F32)
            attended[2 * pair + i] = (summed / summed[:, head_size : head_size + 1]).astype(BF16)
        return carry

    lax.fori_loop(0, heads.shape[1] // 2, pair_step, 0)
    gather_heads(attended, packed, head_size, 64)

    def finish(i, carry):
        rows = pl.ds(pl.multiple_of(i * 128, 128), 128)
        projection = dot_nt(packed[rows, :], out_rows[...])
        updated = (tokens[rows, :].astype(F32) + levels[2:3, :] * projection).astype(BF16)
        for d in range(8):
            for j in range(residual.shape[1] // 16):
                residual[8 * i + d, 16 * j : 16 * j + 16, :] = updated[
                    16 * d : 16 * d + 16, LANES * j : LANES * (j + 1)
                ]
        return carry

    lax.fori_loop(0, row_count // 128, finish, 0)


def temporal_kernel(head_size, received, levels, gains, allowed, w_final, gathered, predicted,
                    landing, heads, out_rows, normed, attended, packed, by_slot, sem):
    arriving = pltpu.make_async_copy(gathered.at[:, 1], landing, sem)
    arriving.start()
    frames = received.shape[0]
    locations = 16
    row_count, width = normed.shape

    def by_frame(b, carry):
        rows = pl.ds(pl.multiple_of(b * locations, 16), locations)
        for j in range(width // LANES):
            packed[rows, LANES * j : LANES * (j + 1)] = received[b, 16 * j : 16 * j + 16, :]
        return carry

    lax.fori_loop(0, frames, by_frame, 0)
    row = lax.broadcasted_iota(jnp.int32, (row_count, row_count), 0)
    column = lax.broadcasted_iota(jnp.int32, (row_count, row_count), 1)
    source = (row % frames) * locations + row // frames
    moved = (column == source).astype(F32).astype(BF16)
    by_slot[...] = jnp.dot(moved, packed[...], preferred_element_type=F32).astype(BF16)
    modulate_rows(by_slot, normed, levels[4:5, :], levels[3:4, :], 64)
    arriving.wait()
    lay_out_weights(landing, heads, out_rows, head_size)
    ones_column = lax.broadcasted_iota(jnp.int32, (row_count, LANES), 1) == head_size
    factor = math.log2(math.e) / math.sqrt(head_size)

    def pair_step(pair, carry):
        queries, keys, values = project_pair(normed, heads, pair)
        for i in range(2):
            lanes = slice(i * LANES, (i + 1) * LANES)
            query = unit_heads(queries[:, lanes], gains[2:3, :], head_size, factor)
            key = unit_heads(keys[:, lanes], gains[3:4, :], head_size, 1.0)
            value = jnp.where(ones_column, 1.0, values[:, lanes]).astype(BF16)
            for start in range(0, row_count, TEMPORAL_ROWS):
                rows = slice(start, start + TEMPORAL_ROWS)
                unnormed = (jnp.exp2(dot_nt(query[rows], key[rows])) * allowed[...]).astype(BF16)
                summed = jnp.dot(unnormed, value[rows], preferred_element_type=F32)
                attended[2 * pair + i, rows, :] = (summed / summed[:, head_size : head_size + 1]).astype(BF16)
        return carry

    lax.fori_loop(0, heads.shape[1] // 2, pair_step, 0)
    gather_heads(attended, packed, head_size, 64)

    def finish(i, carry):
        rows = pl.ds(pl.multiple_of(i * 128, 128), 128)
        projection = dot_nt(packed[rows, :], out_rows[...])
        updated = by_slot[rows, :].astype(F32) + levels[5:6, :] * projection
        normed[rows, :] = layer_norm(updated).astype(BF16)
        return carry

    lax.fori_loop(0, row_count // 128, finish, 0)
    predicted[...] = dot_nt(w_final[...], normed[...])


def weight_scratch(shards, shard_rows, rows, width, head_size):
    head_count = width // head_size
    return [
        pltpu.VMEM((shards, shard_rows, width), BF16),
        pltpu.VMEM((3, head_count, LANES, width), BF16),
        pltpu.VMEM((width, width), BF16),
        pltpu.VMEM((rows, width), BF16),
        pltpu.VMEM((head_count, rows, LANES), BF16),
        pltpu.VMEM((rows, width), BF16),
    ]


def body(
    tokens,
    modulation,
    w_qkv_s,
    w_out_s,
    w_qkv_t,
    w_out_t,
    w_final,
    norm_gains,
    clip_tokens,
    block_clip,
):
    rows, width = tokens.shape[1:]
    head_size = norm_gains.shape[1]
    frames = block_clip.shape[0]
    seq = lax.axis_size("seq")
    locations = rows // seq
    position = lax.axis_index("seq")
    branch_index = lax.axis_index("cfg")
    levels = modulation[0]
    member = block_clip[:, None] == jnp.arange(clip_tokens.shape[0], dtype=jnp.int32)[None, :]
    lengths = jnp.sum(jnp.where(member, clip_tokens[None, :], 0), axis=1)
    own_length = lax.dynamic_slice_in_dim(lengths, position, 1)
    gains = jnp.pad(norm_gains, ((0, 0), (0, LANES - head_size)))
    slot_of = jnp.arange(TEMPORAL_ROWS, dtype=jnp.int32) // frames
    clip_of = jnp.tile(block_clip, TEMPORAL_ROWS // frames)
    allowed = ((slot_of[:, None] == slot_of[None, :]) & (clip_of[:, None] == clip_of[None, :])).astype(F32)

    own_shard = jnp.stack(
        [
            jnp.concatenate([w_qkv_s.T, w_out_s.T], axis=0),
            jnp.concatenate([w_qkv_t.T, w_out_t.T], axis=0),
        ]
    )
    shard_rows = own_shard.shape[1]
    gathered = lax.all_gather(own_shard, ("seq", "cfg"), axis=0, tiled=False)
    shards = gathered.shape[0]
    params = pltpu.CompilerParams(vmem_limit_bytes=58 * 2**20)
    vmem = pl.BlockSpec(memory_space=pltpu.VMEM)
    smem = pl.BlockSpec(memory_space=pltpu.SMEM)
    anywhere = pl.BlockSpec(memory_space=pl.ANY)
    tile_rows = locations * width // LANES
    scratch = weight_scratch(shards, shard_rows, rows, width, head_size)
    residual = pl.pallas_call(
        functools.partial(spatial_kernel, head_size),
        out_shape=jax.ShapeDtypeStruct((seq, tile_rows, LANES), BF16),
        in_specs=[smem, vmem, vmem, vmem, anywhere],
        out_specs=vmem,
        scratch_shapes=scratch + [pltpu.SemaphoreType.DMA],
        compiler_params=params,
        name="spatial",
    )(own_length, tokens[0], levels, gains, gathered)
    received = lax.all_to_all(residual, "seq", split_axis=0, concat_axis=0, tiled=True)
    predicted = pl.pallas_call(
        functools.partial(temporal_kernel, head_size),
        out_shape=jax.ShapeDtypeStruct((w_final.shape[1], rows), F32),
        in_specs=[vmem, vmem, vmem, vmem, vmem, anywhere],
        out_specs=vmem,
        scratch_shapes=scratch + [pltpu.VMEM((rows, width), BF16), pltpu.SemaphoreType.DMA],
        compiler_params=params,
        name="temporal",
    )(received, levels, gains, allowed, w_final.T, gathered)

    half = predicted.shape[0] // 2
    outgoing = lax.dynamic_slice_in_dim(predicted, (1 - branch_index) * half, half, 0)
    other = lax.ppermute(outgoing, "cfg", [(0, 1), (1, 0)])
    own_part = lax.dynamic_slice_in_dim(predicted, branch_index * half, half, 0)
    conditional = jnp.where(branch_index == 0, own_part, other)
    unconditional = jnp.where(branch_index == 0, other, own_part)
    guided = (unconditional + 7.0 * (conditional - unconditional)).reshape(half, locations, frames)
    location_ids = position * locations + jnp.arange(locations, dtype=jnp.int32)
    inside = location_ids[:, None] < lengths[None, :]
    return jnp.where(inside[None], guided, 0.0).transpose(2, 1, 0)


def solution(mesh):
    in_specs = (
        P(("rep", "seq"), None, None),
        P("cfg", None, None),
        P(None, ("seq", "cfg")),
        P(None, ("seq", "cfg")),
        P(None, ("seq", "cfg")),
        P(None, ("seq", "cfg")),
        P(),
        P(),
        P("rep"),
        P("rep"),
    )
    out_specs = P("rep", "seq", "cfg")
    return jax.shard_map(body, mesh=mesh, in_specs=in_specs, out_specs=out_specs, check_vma=False)
```

```python
import functools
import math

import jax
import jax.numpy as jnp
from jax import lax
from jax.experimental import pallas as pl
from jax.experimental.pallas import tpu as pltpu
from jax.sharding import PartitionSpec as P

BF16 = jnp.bfloat16
F32 = jnp.float32
LANES = 128
TEMPORAL_ROWS = 256
X_RING, Z_RING, SPLIT = 4, 8, 384
X_SLOTS = (0, -1, 1, 2)
Z_SLOTS = (0, -1, -2, -3, 1, 2, 3, 4)

def swap_cores(array):
    return lax.ppermute(array, "cfg", [(0, 1), (1, 0)])


def plane_step(array, along_x, far=1):
    pairs = []
    for x in range(X_RING):
        for z in range(Z_RING):
            for core in range(2):
                by = (1 - 2 * core) * far
                to = ((x + by) % X_RING, z) if along_x else (x, (z + by) % Z_RING)
                pairs.append((2 * (x * Z_RING + z) + core, 2 * (to[0] * Z_RING + to[1]) + core))
    return lax.ppermute(array, ("seq", "cfg"), pairs)


def replica_step(array):
    size = lax.axis_size("rep")
    pairs = []
    for y in range(size):
        for core in range(2):
            pairs.append((2 * y + core, 2 * ((y + 1 - 2 * core) % size) + core))
    return lax.ppermute(array, ("rep", "cfg"), pairs)


def in_core_order(core, first, second):
    return jnp.where(core == 0, first, second), jnp.where(core == 0, second, first)


def after(array, earlier):
    return array + earlier[(0,) * earlier.ndim] * jnp.zeros((), array.dtype)


def spread_in_plane(own, core):
    pair = jnp.stack(in_core_order(core, own, swap_cores(own)))
    first, second = pair[:, :, :SPLIT], pair[:, :, SPLIT:]

    def own_half(parts):
        return lax.dynamic_index_in_dim(parts, core, 0, keepdims=True)

    near = [plane_step(second, False, far) for far in (1, 2, 3)]
    near.append(plane_step(own_half(second), False, 4))
    mine = jnp.concatenate([plane_step(first, True), plane_step(own_half(first), True, 2)])
    started = mine
    mine = after(mine, near[3])
    theirs = swap_cores(mine)
    low, high = in_core_order(core, mine[:2], theirs[:2])
    opposite = jnp.concatenate(in_core_order(core, mine[2:], theirs[2:]))
    row = [first, low, high, opposite]
    mine = after(jnp.concatenate(near), started)
    theirs = swap_cores(mine)
    low, high = in_core_order(core, mine[:6], theirs[:6])
    opposite = jnp.concatenate(in_core_order(core, mine[6:], theirs[6:]))
    ring = jnp.concatenate([second, low, high, opposite]).reshape((Z_RING,) + second.shape)
    row = after(jnp.stack(row), theirs)
    across = plane_step(ring, True)
    beyond = plane_step(lax.dynamic_slice_in_dim(across, 4 * core, 4, 0), True)
    rows = [row]
    for hop in range(3):
        rows.append(plane_step(after(rows[-1], across) if hop == 2 else rows[-1], False))
    rows.append(plane_step(lax.dynamic_slice_in_dim(rows[3], 2 * core, 2, 0), False))
    rows += [swap_cores(part) for part in rows[1:]]
    return rows, [ring, across, beyond, swap_cores(across), swap_cores(beyond)]


def pick(table, index):
    found = table[-1]
    for i in range(len(table) - 1):
        found = jnp.where(index == i, table[i], found)
    return found


def plane_copies(place, rows, rings, landing, sem):
    x, z, core = place[0], place[1], place[2]
    sign = 1 - 2 * core
    rest = landing.shape[2] - SPLIT
    copies = []

    def to_landing(part, dx, dz, columns):
        shard = 2 * (lax.rem(x + dx + X_RING, X_RING) * Z_RING + lax.rem(z + dz + Z_RING, Z_RING))
        copies.append(pltpu.make_async_copy(part, landing.at[pl.ds(shard, 2), :, columns], sem))

    for k in range(9):
        hop = k if k < 5 else k - 4
        dz = -sign * hop if k < 5 else sign * hop
        for j in range(rows[k].shape[0]):
            dx = X_SLOTS[j] if hop < 4 else pick(X_SLOTS, (2 * core if k < 5 else 2 - 2 * core) + j)
            to_landing(rows[k].at[j], dx, dz, pl.ds(0, SPLIT))
    for part, dx, start in zip(rings, (0, -sign, 2, sign, 2), (0, 0, 4 * core, 0, 4 - 4 * core)):
        for j in range(part.shape[0]):
            dz = Z_SLOTS[j] if part.shape[0] == Z_RING else pick(Z_SLOTS, start + j)
            to_landing(part.at[j], dx, dz, pl.ds(SPLIT, rest))
    return copies


def replica_copies(place, parts, landing, sem):
    core, y = place[2], place[3]
    size = landing.shape[0]
    sign = 1 - 2 * core
    held, mine, theirs, mine_far, theirs_far = parts
    far = mine_far.shape[0]

    def to(part, dy, start=None):
        slot = landing.at[lax.rem(y + dy + size, size)]
        return pltpu.make_async_copy(part, slot if start is None else slot.at[pl.ds(start, far)], sem)

    return [
        to(held, 0),
        to(mine, -sign),
        to(theirs, sign),
        to(mine_far, 2, far * core),
        to(theirs_far, 2, far - far * core),
    ]


def dot_over(left, right, left_dim, right_dim):
    return lax.dot_general(
        left, right, (((left_dim,), (right_dim,)), ((), ())), preferred_element_type=F32
    )


def layer_norm(values_in, axis):
    average = jnp.mean(values_in, axis=axis, keepdims=True)
    centred = values_in - average
    variance = jnp.mean(centred * centred, axis=axis, keepdims=True)
    return centred * lax.rsqrt(variance + 1e-06)


def lay_out_weights(landing, columns, out_rows, head_size):
    share = 3 * head_size // 4

    def group(g, carry):
        parts = [landing[8 * g + i] for i in range(8)]
        for target, rows in (
            (columns, [part[:share] for part in parts]),
            (out_rows, [part[share:] for part in parts]),
        ):
            size = 8 * rows[0].shape[0]
            target[pl.ds(pl.multiple_of(g * size, 16), size), :] = jnp.concatenate(rows, axis=0)
        return carry

    lax.fori_loop(0, landing.shape[0] // 8, group, 0)


def lay_out_quarters(landing, columns, out_rows, head_size):
    quarter = head_size // 4

    def group(g, carry):
        for target, kinds in ((columns, (0, 1, 2)), (out_rows, (3,))):
            rows = [landing[kind, 8 * g + i][:quarter] for i in range(8) for kind in kinds]
            size = quarter * len(rows)
            target[pl.ds(pl.multiple_of(g * size, 16), size), :] = jnp.concatenate(rows, axis=0)
        return carry

    lax.fori_loop(0, landing.shape[1] // 8, group, 0)


def project(columns, normed, projected):
    width = normed.shape[0]

    def kind(i, carry):
        rows = pl.ds(pl.multiple_of(i * width, 16), width)
        projected[rows, :] = jnp.dot(columns[rows, :], normed[...], preferred_element_type=F32)
        return carry

    lax.fori_loop(0, 3, kind, 0)


def unit_heads(head, gain_column):
    total = jnp.sum(head * head, axis=0, keepdims=True)
    return (head * lax.rsqrt(total / head.shape[0] + 1e-06) * gain_column).astype(BF16)


def attend(projected, attended, gains, first_gain, inside, allowed, head_size):
    width = attended.shape[0]
    row_count = attended.shape[1]
    block = row_count if allowed is None else allowed.shape[0]
    factor = math.log2(math.e) / math.sqrt(head_size)
    query_gain = gains[:, first_gain : first_gain + 1] * factor
    key_gain = gains[:, first_gain + 1 : first_gain + 2]
    ones = jnp.ones((1, row_count), F32)
    blank = jnp.zeros((7, row_count), F32)

    def head(h):
        def part(kind):
            return projected[pl.ds(pl.multiple_of(kind * width + h * head_size, 8), head_size), :]

        query = unit_heads(part(0), query_gain)
        key = unit_heads(part(1), key_gain)
        value = jnp.concatenate([part(2), ones, blank], axis=0)
        if inside is not None:
            value = jnp.where(inside, value, 0.0)
        value = value.astype(BF16)
        found = []
        for start in range(0, row_count, block):
            tokens = slice(start, start + block)
            unnormed = jnp.exp2(dot_over(key[:, tokens], query[:, tokens], 0, 0))
            if allowed is not None:
                unnormed = unnormed * allowed[...]
            summed = jnp.dot(value[:, tokens], unnormed.astype(BF16), preferred_element_type=F32)
            found.append(summed[:head_size] / summed[head_size : head_size + 1])
        return jnp.concatenate(found, axis=1) if len(found) > 1 else found[0]

    def pair(p, carry):
        both = jnp.concatenate([head(2 * p), head(2 * p + 1)], axis=0)
        rows = pl.ds(pl.multiple_of(2 * head_size * p, 16), 2 * head_size)
        attended[rows, :] = both.astype(BF16)
        return carry

    lax.fori_loop(0, width // (2 * head_size), pair, 0)


def spatial_kernel(head_size, place, length_ref, tokens, levels, gains, *refs):
    rows, rings = refs[:9], refs[9:14]
    residual, landing, columns, out_rows, normed, projected, attended, sem = refs[14:]
    arriving = plane_copies(place, rows, rings, landing, sem)
    for copy in arriving:
        copy.start()
    row_count, width = tokens.shape
    for start in range(0, row_count, LANES):
        chunk = slice(start, start + LANES)
        values_in = layer_norm(tokens[chunk, :].astype(F32), 1) * (1.0 + levels[1:2, :]) + levels[0:1, :]
        normed[:, chunk] = values_in.astype(BF16).T
    for copy in arriving:
        copy.wait()
    lay_out_weights(landing, columns, out_rows, head_size)
    project(columns, normed, projected)
    inside = lax.broadcasted_iota(jnp.int32, (head_size + 8, row_count), 1) < length_ref[0]
    attend(projected, attended, gains, 0, inside, None, head_size)
    for start in range(0, row_count, 256):
        chunk = slice(start, start + 256)
        projection = dot_over(attended[:, chunk], out_rows[...], 0, 1)
        updated = (tokens[chunk, :].astype(F32) + levels[2:3, :] * projection).astype(BF16)
        for d in range(16):
            for j in range(residual.shape[1] // 16):
                residual[start // 16 + d, 16 * j : 16 * j + 16, :] = updated[
                    16 * d : 16 * d + 16, LANES * j : LANES * (j + 1)
                ]


def temporal_kernel(head_size, place, received, levels, gains, allowed, w_final, *refs):
    predicted, landing, columns, out_rows, normed, projected, attended, by_frame, by_slot, sem = refs[5:]
    arriving = replica_copies(place, refs[:5], landing, sem)
    for copy in arriving:
        copy.start()
    frames = received.shape[0]
    width, row_count = normed.shape
    locations = row_count // frames

    def unpack(b, carry):
        rows = pl.ds(pl.multiple_of(b * locations, 16), locations)
        for j in range(width // LANES):
            by_frame[rows, LANES * j : LANES * (j + 1)] = received[b, 16 * j : 16 * j + 16, :]
        return carry

    lax.fori_loop(0, frames, unpack, 0)
    row = lax.broadcasted_iota(jnp.int32, (row_count, row_count), 0)
    column = lax.broadcasted_iota(jnp.int32, (row_count, row_count), 1)
    moved = (row == (column % frames) * locations + column // frames).astype(F32).astype(BF16)
    by_slot[...] = dot_over(by_frame[...], moved, 0, 0).astype(BF16)
    for start in range(0, row_count, LANES):
        chunk = slice(start, start + LANES)
        values_in = layer_norm(by_slot[:, chunk].astype(F32), 0)
        normed[:, chunk] = (values_in * (1.0 + levels[:, 4:5]) + levels[:, 3:4]).astype(BF16)
    for copy in arriving:
        copy.wait()
    lay_out_quarters(landing, columns, out_rows, head_size)
    project(columns, normed, projected)
    attend(projected, attended, gains, 2, None, allowed, head_size)
    projected[0:width, :] = jnp.dot(out_rows[...], attended[...], preferred_element_type=F32)
    for start in range(0, row_count, LANES):
        chunk = slice(start, start + LANES)
        updated = by_slot[:, chunk].astype(F32) + levels[:, 5:6] * projected[0:width, chunk]
        normed[:, chunk] = layer_norm(updated, 0).astype(BF16)
    predicted[...] = jnp.dot(w_final[...], normed[...], preferred_element_type=F32)


def weight_scratch(landing_shape, rows, width):
    return [
        pltpu.VMEM(landing_shape, BF16),
        pltpu.VMEM((3 * width, width), BF16),
        pltpu.VMEM((width, width), BF16),
        pltpu.VMEM((width, rows), BF16),
        pltpu.VMEM((3 * width, rows), F32),
        pltpu.VMEM((width, rows), BF16),
    ]


def body(
    tokens,
    modulation,
    w_qkv_s,
    w_out_s,
    w_qkv_t,
    w_out_t,
    w_final,
    norm_gains,
    clip_tokens,
    block_clip,
):
    rows, width = tokens.shape[1:]
    head_size = norm_gains.shape[1]
    frames = block_clip.shape[0]
    seq = lax.axis_size("seq")
    locations = rows // seq
    position = lax.axis_index("seq")
    branch_index = lax.axis_index("cfg")
    levels = modulation[0]
    member = block_clip[:, None] == jnp.arange(clip_tokens.shape[0], dtype=jnp.int32)[None, :]
    lengths = jnp.sum(jnp.where(member, clip_tokens[None, :], 0), axis=1)
    own_length = lax.dynamic_slice_in_dim(lengths, position, 1)
    gains = norm_gains.T
    slot_of = jnp.arange(TEMPORAL_ROWS, dtype=jnp.int32) // frames
    clip_of = jnp.tile(block_clip, TEMPORAL_ROWS // frames)
    allowed = ((slot_of[:, None] == slot_of[None, :]) & (clip_of[:, None] == clip_of[None, :])).astype(F32)

    y = lax.axis_index("rep")
    place = jnp.stack([position // Z_RING, position % Z_RING, branch_index, y]).astype(jnp.int32)
    later = jnp.concatenate([w_qkv_t.T, w_out_t.T], axis=0)
    quarter_rows = later.shape[0] // lax.axis_size("rep")
    own_quarter = lax.dynamic_slice_in_dim(later, y * quarter_rows, quarter_rows, 0)
    own_quarter = jnp.pad(own_quarter, ((0, -quarter_rows % 8), (0, 0)))
    quarter = lax.all_gather(own_quarter, ("seq", "cfg"), axis=0, tiled=False)
    row_parts, ring_parts = spread_in_plane(jnp.concatenate([w_qkv_s.T, w_out_s.T], axis=0), branch_index)
    shards = quarter.shape[0]
    quarter = after(after(quarter, row_parts[4]), ring_parts[2])
    params = pltpu.CompilerParams(vmem_limit_bytes=58 * 2**20)
    vmem = pl.BlockSpec(memory_space=pltpu.VMEM)
    smem = pl.BlockSpec(memory_space=pltpu.SMEM)
    anywhere = pl.BlockSpec(memory_space=pl.ANY)
    tile_rows = locations * width // LANES
    cost = pl.CostEstimate(flops=30_000_000_000, bytes_accessed=20_000_000, transcendentals=0)
    residual = pl.pallas_call(
        functools.partial(spatial_kernel, head_size),
        out_shape=jax.ShapeDtypeStruct((seq, tile_rows, LANES), BF16),
        in_specs=[smem, smem, vmem, vmem, vmem] + [anywhere] * 14,
        out_specs=vmem,
        scratch_shapes=weight_scratch((shards, later.shape[0], width), rows, width)
        + [pltpu.SemaphoreType.DMA],
        compiler_params=params,
        cost_estimate=cost,
        name="spatial",
    )(place, own_length, tokens[0], levels, gains, *row_parts, *ring_parts)
    next_quarter = replica_step(quarter)
    next_quarter = after(next_quarter, residual)
    far_quarter = replica_step(
        lax.dynamic_slice_in_dim(next_quarter, branch_index * (shards // 2), shards // 2, 0)
    )
    quarters = (quarter, next_quarter, swap_cores(next_quarter), far_quarter, swap_cores(far_quarter))
    received = lax.all_to_all(residual, "seq", split_axis=0, concat_axis=0, tiled=True)
    predicted = pl.pallas_call(
        functools.partial(temporal_kernel, head_size),
        out_shape=jax.ShapeDtypeStruct((w_final.shape[1], rows), F32),
        in_specs=[smem, vmem, vmem, vmem, vmem, vmem] + [anywhere] * 5,
        out_specs=vmem,
        scratch_shapes=weight_scratch(
            (lax.axis_size("rep"), shards, quarter.shape[1], width), rows, width
        )
        + [pltpu.VMEM((rows, width), BF16), pltpu.VMEM((width, rows), BF16), pltpu.SemaphoreType.DMA],
        compiler_params=params,
        cost_estimate=cost,
        name="temporal",
    )(place, received, levels.T, gains, allowed, w_final.T, *quarters)

    half = predicted.shape[0] // 2
    outgoing = lax.dynamic_slice_in_dim(predicted, (1 - branch_index) * half, half, 0)
    other = lax.ppermute(outgoing, "cfg", [(0, 1), (1, 0)])
    own_part = lax.dynamic_slice_in_dim(predicted, branch_index * half, half, 0)
    conditional = jnp.where(branch_index == 0, own_part, other)
    unconditional = jnp.where(branch_index == 0, other, own_part)
    guided = (unconditional + 7.0 * (conditional - unconditional)).reshape(half, locations, frames)
    location_ids = position * locations + jnp.arange(locations, dtype=jnp.int32)
    inside = location_ids[:, None] < lengths[None, :]
    return jnp.where(inside[None], guided, 0.0).transpose(2, 1, 0)


def solution(mesh):
    in_specs = (
        P(("rep", "seq"), None, None),
        P("cfg", None, None),
        P(None, ("seq", "cfg")),
        P(None, ("seq", "cfg")),
        P(None, ("seq", "cfg")),
        P(None, ("seq", "cfg")),
        P(),
        P(),
        P("rep"),
        P("rep"),
    )
    out_specs = P("rep", "seq", "cfg")
    return jax.shard_map(body, mesh=mesh, in_specs=in_specs, out_specs=out_specs, check_vma=False)
```

```python
import functools
import math

import jax
import jax.numpy as jnp
from jax import lax
from jax.experimental import pallas as pl
from jax.experimental.pallas import tpu as pltpu
from jax.sharding import PartitionSpec as P

BF16 = jnp.bfloat16
F32 = jnp.float32
LANES = 128
TEMPORAL_ROWS = 256
X_RING, Z_RING, SPLIT = 4, 8, 512
X_SLOTS = (0, -1, 1, 2)
Z_SLOTS = (0, -1, -2, -3, 1, 2, 3, 4)

def swap_cores(array):
    return lax.ppermute(array, "cfg", [(0, 1), (1, 0)])


def plane_step(array, along_x, far=1):
    pairs = []
    for x in range(X_RING):
        for z in range(Z_RING):
            for core in range(2):
                by = (1 - 2 * core) * far
                to = ((x + by) % X_RING, z) if along_x else (x, (z + by) % Z_RING)
                pairs.append((2 * (x * Z_RING + z) + core, 2 * (to[0] * Z_RING + to[1]) + core))
    return lax.ppermute(array, ("seq", "cfg"), pairs)


def in_core_order(core, first, second):
    return jnp.where(core == 0, first, second), jnp.where(core == 0, second, first)


def spread_in_plane(own, core):
    pair = jnp.stack(in_core_order(core, own, swap_cores(own)))
    first, second = pair[:, :, :SPLIT], pair[:, :, SPLIT:]

    def own_half(parts):
        return lax.dynamic_index_in_dim(parts, core, 0, keepdims=True)

    near = [plane_step(second, False, far) for far in (1, 2, 3)]
    near.append(plane_step(own_half(second), False, 4))
    mine = jnp.concatenate([plane_step(first, True), plane_step(own_half(first), True, 2)])
    theirs = swap_cores(mine)
    low, high = in_core_order(core, mine[:2], theirs[:2])
    opposite = jnp.concatenate(in_core_order(core, mine[2:], theirs[2:]))
    rows = [jnp.stack([first, low, high, opposite])]
    for _ in range(3):
        rows.append(plane_step(rows[-1], False))
    mine = jnp.concatenate(near)
    theirs = swap_cores(mine)
    low, high = in_core_order(core, mine[:6], theirs[:6])
    opposite = jnp.concatenate(in_core_order(core, mine[6:], theirs[6:]))
    ring = jnp.concatenate([second, low, high, opposite]).reshape((Z_RING,) + second.shape)
    across = plane_step(ring, True)
    beyond = plane_step(lax.dynamic_slice_in_dim(across, 4 * core, 4, 0), True)
    rows.append(plane_step(lax.dynamic_slice_in_dim(rows[3], 2 * core, 2, 0), False))
    rows += [swap_cores(part) for part in rows[1:]]
    return rows, [ring, across, beyond, swap_cores(across), swap_cores(beyond)]


def pick(table, index):
    found = table[-1]
    for i in range(len(table) - 1):
        found = jnp.where(index == i, table[i], found)
    return found


def plane_copies(rows, rings, landing, sem):
    position, core = lax.axis_index("seq"), lax.axis_index("cfg")
    x, z = position // Z_RING, position % Z_RING
    sign = 1 - 2 * core
    rest = landing.shape[2] - SPLIT
    copies = []

    def to_landing(part, dx, dz, columns):
        shard = 2 * (lax.rem(x + dx + X_RING, X_RING) * Z_RING + lax.rem(z + dz + Z_RING, Z_RING))
        copies.append(pltpu.make_async_copy(part, landing.at[pl.ds(shard, 2), :, columns], sem))

    for k in range(9):
        hop = k if k < 5 else k - 4
        dz = -sign * hop if k < 5 else sign * hop
        for j in range(rows[k].shape[0]):
            dx = X_SLOTS[j] if hop < 4 else pick(X_SLOTS, (2 * core if k < 5 else 2 - 2 * core) + j)
            to_landing(rows[k].at[j], dx, dz, pl.ds(0, SPLIT))
    for part, dx, start in zip(rings, (0, -sign, 2, sign, 2), (0, 0, 4 * core, 0, 4 - 4 * core)):
        for j in range(part.shape[0]):
            dz = Z_SLOTS[j] if part.shape[0] == Z_RING else pick(Z_SLOTS, start + j)
            to_landing(part.at[j], dx, dz, pl.ds(SPLIT, rest))
    return copies


def dot_over(left, right, left_dim, right_dim):
    return lax.dot_general(
        left, right, (((left_dim,), (right_dim,)), ((), ())), preferred_element_type=F32
    )


def layer_norm(values_in, axis):
    average = jnp.mean(values_in, axis=axis, keepdims=True)
    centred = values_in - average
    variance = jnp.mean(centred * centred, axis=axis, keepdims=True)
    return centred * lax.rsqrt(variance + 1e-06)


def lay_out(landing, target, first, count):
    size = 8 * count

    def group(g, carry):
        rows = [landing[8 * g + i][first : first + count] for i in range(8)]
        target[pl.ds(pl.multiple_of(g * size, 16), size), :] = jnp.concatenate(rows, axis=0)
        return carry

    lax.fori_loop(0, landing.shape[0] // 8, group, 0)


def project(columns, normed, projected):
    width = normed.shape[0]

    def kind(i, carry):
        rows = pl.ds(pl.multiple_of(i * width, 16), width)
        projected[rows, :] = jnp.dot(columns[rows, :], normed[...], preferred_element_type=F32)
        return carry

    lax.fori_loop(0, 3, kind, 0)


def unit_heads(head, gain_column):
    total = jnp.sum(head * head, axis=0, keepdims=True)
    return (head * lax.rsqrt(total / head.shape[0] + 1e-06) * gain_column).astype(BF16)


def attend(projected, attended, gains, first_gain, inside, allowed, head_size):
    width = attended.shape[0]
    row_count = attended.shape[1]
    block = row_count if allowed is None else allowed.shape[0]
    factor = math.log2(math.e) / math.sqrt(head_size)
    query_gain = gains[:, first_gain : first_gain + 1] * factor
    key_gain = gains[:, first_gain + 1 : first_gain + 2]
    ones = jnp.ones((1, row_count), F32)
    blank = jnp.zeros((7, row_count), F32)

    def head(h):
        def part(kind):
            return projected[pl.ds(pl.multiple_of(kind * width + h * head_size, 8), head_size), :]

        query = unit_heads(part(0), query_gain)
        key = unit_heads(part(1), key_gain)
        value = jnp.concatenate([part(2), ones, blank], axis=0)
        if inside is not None:
            value = jnp.where(inside, value, 0.0)
        value = value.astype(BF16)
        found = []
        for start in range(0, row_count, block):
            tokens = slice(start, start + block)
            unnormed = jnp.exp2(dot_over(key[:, tokens], query[:, tokens], 0, 0))
            if allowed is not None:
                unnormed = unnormed * allowed[...]
            summed = jnp.dot(value[:, tokens], unnormed.astype(BF16), preferred_element_type=F32)
            found.append(summed[:head_size] / summed[head_size : head_size + 1])
        return jnp.concatenate(found, axis=1) if len(found) > 1 else found[0]

    def pair(p, carry):
        both = jnp.concatenate([head(2 * p), head(2 * p + 1)], axis=0)
        rows = pl.ds(pl.multiple_of(2 * head_size * p, 16), 2 * head_size)
        attended[rows, :] = both.astype(BF16)
        return carry

    lax.fori_loop(0, width // (2 * head_size), pair, 0)


def spatial_kernel(head_size, clip_tokens, block_clip, tokens, levels, gains, *refs):
    rows, rings = refs[:9], refs[9:14]
    attended, landing, columns, normed, projected, sem = refs[14:]
    arriving = plane_copies(rows, rings, landing, sem)
    for copy in arriving:
        copy.start()
    row_count = tokens.shape[0]
    for start in range(0, row_count, LANES):
        chunk = slice(start, start + LANES)
        values_in = layer_norm(tokens[chunk, :].astype(F32), 1) * (1.0 + levels[1]) + levels[0]
        normed[:, chunk] = values_in.astype(BF16).T
    for copy in arriving:
        copy.wait()
    lay_out(landing, columns, 0, 3 * head_size // 4)
    project(columns, normed, projected)
    length = clip_tokens[block_clip[lax.axis_index("seq")]]
    inside = lax.broadcasted_iota(jnp.int32, (head_size + 8, row_count), 1) < length
    attend(projected, attended, gains, 0, inside, None, head_size)


def mixing_kernel(head_size, tokens, levels, attended, gathered, residual, landing, out_rows, sem):
    first, kept = landing.shape[1] * 2, landing.shape[1]
    arriving = pltpu.make_async_copy(gathered.at[:, pl.ds(first, kept), :], landing, sem)
    arriving.start()
    arriving.wait()
    lay_out(landing, out_rows, head_size - first, head_size // 4)
    for start in range(0, tokens.shape[0], 256):
        chunk = slice(start, start + 256)
        projection = dot_over(attended[:, chunk], out_rows[...], 0, 1)
        updated = (tokens[chunk, :].astype(F32) + levels[2] * projection).astype(BF16)
        for d in range(16):
            for j in range(residual.shape[1] // 16):
                residual[start // 16 + d, 16 * j : 16 * j + 16, :] = updated[
                    16 * d : 16 * d + 16, LANES * j : LANES * (j + 1)
                ]


def temporal_kernel(head_size, received, levels, gains, allowed, w_final, gathered, predicted,
                    landing, columns, normed, projected, out_rows, attended, by_frame, by_slot, sem):
    arriving = pltpu.make_async_copy(gathered.at[:, pl.ds(0, landing.shape[1]), :], landing, sem)
    arriving.start()
    frames = received.shape[0]
    width, row_count = normed.shape
    locations = row_count // frames

    def unpack(b, carry):
        rows = pl.ds(pl.multiple_of(b * locations, 16), locations)
        for j in range(width // LANES):
            by_frame[rows, LANES * j : LANES * (j + 1)] = received[b, 16 * j : 16 * j + 16, :]
        return carry

    lax.fori_loop(0, frames, unpack, 0)
    row = lax.broadcasted_iota(jnp.int32, (row_count, row_count), 0)
    column = lax.broadcasted_iota(jnp.int32, (row_count, row_count), 1)
    moved = (row == (column % frames) * locations + column // frames).astype(F32).astype(BF16)
    by_slot[...] = dot_over(by_frame[...], moved, 0, 0).astype(BF16)
    for start in range(0, row_count, LANES):
        chunk = slice(start, start + LANES)
        values_in = layer_norm(by_slot[:, chunk].astype(F32), 0)
        normed[:, chunk] = (values_in * (1.0 + levels[:, 4:5]) + levels[:, 3:4]).astype(BF16)
    arriving.wait()
    share = 3 * head_size // 4
    lay_out(landing, columns, 0, share)
    lay_out(landing, out_rows, share, head_size // 4)
    project(columns, normed, projected)
    attend(projected, attended, gains, 2, None, allowed, head_size)
    projected[0:width, :] = jnp.dot(out_rows[...], attended[...], preferred_element_type=F32)
    for start in range(0, row_count, LANES):
        chunk = slice(start, start + LANES)
        updated = by_slot[:, chunk].astype(F32) + levels[:, 5:6] * projected[0:width, chunk]
        normed[:, chunk] = layer_norm(updated, 0).astype(BF16)
    predicted[...] = jnp.dot(w_final[...], normed[...], preferred_element_type=F32)


def projection_scratch(landing_shape, rows, width):
    return [
        pltpu.VMEM(landing_shape, BF16),
        pltpu.VMEM((3 * width, width), BF16),
        pltpu.VMEM((width, rows), BF16),
        pltpu.VMEM((3 * width, rows), F32),
    ]


def body(
    tokens,
    modulation,
    w_qkv_s,
    w_out_s,
    w_qkv_t,
    w_out_t,
    w_final,
    norm_gains,
    clip_tokens,
    block_clip,
):
    rows, width = tokens.shape[1:]
    head_size = norm_gains.shape[1]
    frames = block_clip.shape[0]
    seq = lax.axis_size("seq")
    locations = rows // seq
    position = lax.axis_index("seq")
    branch_index = lax.axis_index("cfg")
    levels = modulation.transpose(1, 0, 2)
    member = block_clip[:, None] == jnp.arange(clip_tokens.shape[0], dtype=jnp.int32)[None, :]
    lengths = jnp.sum(jnp.where(member, clip_tokens[None, :], 0), axis=1)
    gains = norm_gains.T
    slot_of = jnp.arange(TEMPORAL_ROWS, dtype=jnp.int32) // frames
    clip_of = jnp.tile(block_clip, TEMPORAL_ROWS // frames)
    allowed = ((slot_of[:, None] == slot_of[None, :]) & (clip_of[:, None] == clip_of[None, :])).astype(F32)

    first_rows = jnp.pad(w_qkv_s.T, ((0, -w_qkv_s.shape[1] % 8), (0, 0)))
    later_rows = jnp.concatenate([w_qkv_t.T, w_out_t.T, w_out_s.T], axis=0)
    later_rows = jnp.pad(later_rows, ((0, -later_rows.shape[0] % 32), (0, 0)))
    gathered = lax.all_gather(later_rows, ("seq", "cfg"), axis=0, tiled=False)
    shards = gathered.shape[0]
    row_parts, ring_parts = spread_in_plane(first_rows, branch_index)
    params = pltpu.CompilerParams(vmem_limit_bytes=58 * 2**20)
    vmem = pl.BlockSpec(memory_space=pltpu.VMEM)
    smem = pl.BlockSpec(memory_space=pltpu.SMEM)
    anywhere = pl.BlockSpec(memory_space=pl.ANY)
    tile_rows = locations * width // LANES
    cost = pl.CostEstimate(flops=20_000_000_000, bytes_accessed=20_000_000, transcendentals=0)
    attended = pl.pallas_call(
        functools.partial(spatial_kernel, head_size),
        out_shape=jax.ShapeDtypeStruct((width, rows), BF16),
        in_specs=[smem, smem, vmem, vmem, vmem] + [anywhere] * 14,
        out_specs=vmem,
        scratch_shapes=projection_scratch((shards,) + first_rows.shape, rows, width)
        + [pltpu.SemaphoreType.DMA],
        compiler_params=params,
        cost_estimate=cost,
        name="spatial",
    )(clip_tokens, block_clip, tokens[0], levels, gains, *row_parts, *ring_parts)
    residual = pl.pallas_call(
        functools.partial(mixing_kernel, head_size),
        out_shape=jax.ShapeDtypeStruct((seq, tile_rows, LANES), BF16),
        in_specs=[vmem, vmem, vmem, anywhere],
        out_specs=vmem,
        scratch_shapes=[
            pltpu.VMEM((shards, 32, width), BF16),
            pltpu.VMEM((width, width), BF16),
            pltpu.SemaphoreType.DMA,
        ],
        compiler_params=params,
        cost_estimate=cost,
        name="mixing",
    )(tokens[0], levels, attended, gathered)
    received = lax.all_to_all(residual, "seq", split_axis=0, concat_axis=0, tiled=True)
    predicted = pl.pallas_call(
        functools.partial(temporal_kernel, head_size),
        out_shape=jax.ShapeDtypeStruct((w_final.shape[1], rows), F32),
        in_specs=[vmem] * 5 + [anywhere],
        out_specs=vmem,
        scratch_shapes=projection_scratch((shards, 80, width), rows, width)
        + [
            pltpu.VMEM((width, width), BF16),
            pltpu.VMEM((width, rows), BF16),
            pltpu.VMEM((rows, width), BF16),
            pltpu.VMEM((width, rows), BF16),
            pltpu.SemaphoreType.DMA,
        ],
        compiler_params=params,
        cost_estimate=cost,
        name="temporal",
    )(received, modulation[0].T, gains, allowed, w_final.T, gathered)

    half = predicted.shape[0] // 2
    outgoing = lax.dynamic_slice_in_dim(predicted, (1 - branch_index) * half, half, 0)
    other = lax.ppermute(outgoing, "cfg", [(0, 1), (1, 0)])
    own_part = lax.dynamic_slice_in_dim(predicted, branch_index * half, half, 0)
    conditional = jnp.where(branch_index == 0, own_part, other)
    unconditional = jnp.where(branch_index == 0, other, own_part)
    guided = (unconditional + 7.0 * (conditional - unconditional)).reshape(half, locations, frames)
    location_ids = position * locations + jnp.arange(locations, dtype=jnp.int32)
    inside = location_ids[:, None] < lengths[None, :]
    return jnp.where(inside[None], guided, 0.0).transpose(2, 1, 0)


def solution(mesh):
    in_specs = (
        P(("rep", "seq"), None, None),
        P("cfg", None, None),
        P(None, ("seq", "cfg")),
        P(None, ("seq", "cfg")),
        P(None, ("seq", "cfg")),
        P(None, ("seq", "cfg")),
        P(),
        P(),
        P("rep"),
        P("rep"),
    )
    out_specs = P("rep", "seq", "cfg")
    return jax.shard_map(body, mesh=mesh, in_specs=in_specs, out_specs=out_specs, check_vma=False)
```

```python
import functools
import math

import jax
import jax.numpy as jnp
from jax import lax
from jax.experimental import pallas as pl
from jax.experimental.pallas import tpu as pltpu
from jax.sharding import PartitionSpec as P

BF16 = jnp.bfloat16
F32 = jnp.float32
LANES = 128
PIECES = 2
X_RING, Z_RING, SPLIT = 4, 8, 512
X_SLOTS = (0, -1, 1, 2)
Z_SLOTS = (0, -1, -2, -3, 1, 2, 3, 4)

def swap_cores(array):
    return lax.ppermute(array, "cfg", [(0, 1), (1, 0)])


def plane_step(array, along_x, far=1):
    pairs = []
    for x in range(X_RING):
        for z in range(Z_RING):
            for core in range(2):
                by = (1 - 2 * core) * far
                to = ((x + by) % X_RING, z) if along_x else (x, (z + by) % Z_RING)
                pairs.append((2 * (x * Z_RING + z) + core, 2 * (to[0] * Z_RING + to[1]) + core))
    return lax.ppermute(array, ("seq", "cfg"), pairs)


def in_core_order(core, first, second):
    return jnp.where(core == 0, first, second), jnp.where(core == 0, second, first)


def spread_in_plane(own, core):
    pair = jnp.stack(in_core_order(core, own, swap_cores(own)))
    first, second = pair[:, :, :SPLIT], pair[:, :, SPLIT:]

    def own_half(parts):
        return lax.dynamic_index_in_dim(parts, core, 0, keepdims=True)

    near = [plane_step(second, False, far) for far in (1, 2, 3)]
    near.append(plane_step(own_half(second), False, 4))
    mine = jnp.concatenate([plane_step(first, True), plane_step(own_half(first), True, 2)])
    theirs = swap_cores(mine)
    low, high = in_core_order(core, mine[:2], theirs[:2])
    opposite = jnp.concatenate(in_core_order(core, mine[2:], theirs[2:]))
    rows = [jnp.stack([first, low, high, opposite])]
    for _ in range(3):
        rows.append(plane_step(rows[-1], False))
    mine = jnp.concatenate(near)
    theirs = swap_cores(mine)
    low, high = in_core_order(core, mine[:6], theirs[:6])
    opposite = jnp.concatenate(in_core_order(core, mine[6:], theirs[6:]))
    ring = jnp.concatenate([second, low, high, opposite]).reshape((Z_RING,) + second.shape)
    across = plane_step(ring, True)
    beyond = plane_step(lax.dynamic_slice_in_dim(across, 4 * core, 4, 0), True)
    rows.append(plane_step(lax.dynamic_slice_in_dim(rows[3], 2 * core, 2, 0), False))
    rows += [swap_cores(part) for part in rows[1:]]
    return rows, [ring, across, beyond, swap_cores(across), swap_cores(beyond)]


def pick(table, index):
    found = table[-1]
    for i in range(len(table) - 1):
        found = jnp.where(index == i, table[i], found)
    return found


def plane_copies(rows, rings, landing, sem):
    position, core = lax.axis_index("seq"), lax.axis_index("cfg")
    x, z = position // Z_RING, position % Z_RING
    sign = 1 - 2 * core
    rest = landing.shape[2] - SPLIT
    copies = []

    def to_landing(part, dx, dz, columns):
        shard = 2 * (lax.rem(x + dx + X_RING, X_RING) * Z_RING + lax.rem(z + dz + Z_RING, Z_RING))
        copies.append(pltpu.make_async_copy(part, landing.at[pl.ds(shard, 2), :, columns], sem))

    for k in range(9):
        hop = k if k < 5 else k - 4
        dz = -sign * hop if k < 5 else sign * hop
        for j in range(rows[k].shape[0]):
            dx = X_SLOTS[j] if hop < 4 else pick(X_SLOTS, (2 * core if k < 5 else 2 - 2 * core) + j)
            to_landing(rows[k].at[j], dx, dz, pl.ds(0, SPLIT))
    for part, dx, start in zip(rings, (0, -sign, 2, sign, 2), (0, 0, 4 * core, 0, 4 - 4 * core)):
        for j in range(part.shape[0]):
            dz = Z_SLOTS[j] if part.shape[0] == Z_RING else pick(Z_SLOTS, start + j)
            to_landing(part.at[j], dx, dz, pl.ds(SPLIT, rest))
    return copies


def dot_over(left, right, left_dim, right_dim):
    return lax.dot_general(
        left, right, (((left_dim,), (right_dim,)), ((), ())), preferred_element_type=F32
    )


def layer_norm(values_in, axis):
    average = jnp.mean(values_in, axis=axis, keepdims=True)
    centred = values_in - average
    variance = jnp.mean(centred * centred, axis=axis, keepdims=True)
    return centred * lax.rsqrt(variance + 1e-06)


def lay_out(landing, target, first, count):
    size = 8 * count

    def group(g, carry):
        rows = [landing[8 * g + i][first : first + count] for i in range(8)]
        target[pl.ds(pl.multiple_of(g * size, 16), size), :] = jnp.concatenate(rows, axis=0)
        return carry

    lax.fori_loop(0, landing.shape[0] // 8, group, 0)


def project(columns, normed, projected):
    width = normed.shape[0]

    def kind(i, carry):
        rows = pl.ds(pl.multiple_of(i * width, 16), width)
        projected[rows, :] = jnp.dot(columns[rows, :], normed[...], preferred_element_type=F32)
        return carry

    lax.fori_loop(0, 3, kind, 0)


def unit_heads(head, gain_column):
    total = jnp.sum(head * head, axis=0, keepdims=True)
    return (head * lax.rsqrt(total / head.shape[0] + 1e-06) * gain_column).astype(BF16)


def attend(projected, attended, gains, first_gain, inside, allowed, head_size):
    width = attended.shape[0]
    row_count = attended.shape[1]
    block = row_count if allowed is None else allowed.shape[0]
    factor = math.log2(math.e) / math.sqrt(head_size)
    query_gain = gains[:, first_gain : first_gain + 1] * factor
    key_gain = gains[:, first_gain + 1 : first_gain + 2]
    ones = jnp.ones((1, row_count), F32)
    blank = jnp.zeros((7, row_count), F32)

    def head(h):
        def part(kind):
            return projected[pl.ds(pl.multiple_of(kind * width + h * head_size, 8), head_size), :]

        query = unit_heads(part(0), query_gain)
        key = unit_heads(part(1), key_gain)
        value = jnp.concatenate([part(2), ones, blank], axis=0)
        if inside is not None:
            value = jnp.where(inside, value, 0.0)
        value = value.astype(BF16)
        found = []
        for start in range(0, row_count, block):
            tokens = slice(start, start + block)
            unnormed = jnp.exp2(dot_over(key[:, tokens], query[:, tokens], 0, 0))
            if allowed is not None:
                unnormed = unnormed * allowed[...]
            summed = jnp.dot(value[:, tokens], unnormed.astype(BF16), preferred_element_type=F32)
            found.append(summed[:head_size] / summed[head_size : head_size + 1])
        return jnp.concatenate(found, axis=1) if len(found) > 1 else found[0]

    def pair(p, carry):
        both = jnp.concatenate([head(2 * p), head(2 * p + 1)], axis=0)
        rows = pl.ds(pl.multiple_of(2 * head_size * p, 16), 2 * head_size)
        attended[rows, :] = both.astype(BF16)
        return carry

    lax.fori_loop(0, width // (2 * head_size), pair, 0)


def piece_rows(values_in, piece):
    rows, width = values_in.shape
    split = values_in.reshape(rows // (8 * PIECES), PIECES, 8, width)
    return split[:, piece].reshape(rows // PIECES, width)


def spatial_kernel(head_size, clip_tokens, block_clip, tokens, levels, gains, *refs):
    rows, rings = refs[:9], refs[9:14]
    attended, landing, columns, normed, projected, sem = refs[14:]
    arriving = plane_copies(rows, rings, landing, sem)
    for copy in arriving:
        copy.start()
    row_count = tokens.shape[0]
    for start in range(0, row_count, 2 * LANES):
        chunk = slice(start, start + 2 * LANES)
        values_in = layer_norm(tokens[chunk, :].astype(F32), 1) * (1.0 + levels[1]) + levels[0]
        for piece in range(PIECES):
            first = (piece * row_count + start) // PIECES
            normed[:, first : first + LANES] = piece_rows(values_in, piece).astype(BF16).T
    for copy in arriving:
        copy.wait()
    lay_out(landing, columns, 0, 3 * head_size // 4)
    project(columns, normed, projected)
    length = clip_tokens[block_clip[lax.axis_index("seq")]]
    lane = lax.broadcasted_iota(jnp.int32, (head_size + 8, row_count), 1)
    place = lane % (row_count // PIECES)
    inside = place // 8 * (8 * PIECES) + lane // (row_count // PIECES) * 8 + place % 8 < length
    attend(projected, attended, gains, 0, inside, None, head_size)


def mixing_kernel(head_size, tokens, levels, attended, gathered, *refs):
    pieces, (landing, out_rows, sem) = refs[:PIECES], refs[PIECES:]
    first, kept = landing.shape[1] * 2, landing.shape[1]
    arriving = pltpu.make_async_copy(gathered.at[:, pl.ds(first, kept), :], landing, sem)
    arriving.start()
    arriving.wait()
    lay_out(landing, out_rows, head_size - first, head_size // 4)
    row_count, width = tokens.shape
    size = row_count // PIECES
    for piece in range(PIECES):
        projection = dot_over(attended[:, piece * size : (piece + 1) * size], out_rows[...], 0, 1)
        for start in range(0, size, LANES):
            own = piece_rows(tokens[start * PIECES : (start + LANES) * PIECES, :].astype(F32), piece)
            updated = own + levels[2] * projection[start : start + LANES]
            for d in range(LANES // 8):
                rows = slice(8 * d, 8 * d + 8)
                tiles = [updated[rows, LANES * j : LANES * (j + 1)] for j in range(width // LANES)]
                pieces[piece][start // 8 + d] = jnp.concatenate(tiles, axis=0).astype(BF16)


def prepare_kernel(head_size, gathered, columns, out_rows, landing, sem):
    arriving = pltpu.make_async_copy(gathered.at[:, pl.ds(0, landing.shape[1]), :], landing, sem)
    arriving.start()
    arriving.wait()
    share = 3 * head_size // 4
    lay_out(landing, columns, 0, share)
    lay_out(landing, out_rows, share, head_size // 4)


def temporal_kernel(head_size, received, levels, gains, allowed, w_final, held_columns, held_rows, predicted,
                    columns, normed, projected, out_rows, attended, by_frame, by_slot, sems):
    arriving = [
        pltpu.make_async_copy(held_columns, columns, sems.at[0]),
        pltpu.make_async_copy(held_rows, out_rows, sems.at[1]),
    ]
    for copy in arriving:
        copy.start()
    frames = received.shape[0]
    width, row_count = normed.shape
    locations = row_count // frames

    def unpack(b, carry):
        rows = pl.ds(pl.multiple_of(b * locations, 8), locations)
        values_in = received[b].astype(F32)
        for j in range(width // LANES):
            by_frame[rows, LANES * j : LANES * (j + 1)] = values_in[locations * j : locations * (j + 1)]
        return carry

    lax.fori_loop(0, frames, unpack, 0)
    row = lax.broadcasted_iota(jnp.int32, (row_count, row_count), 0)
    column = lax.broadcasted_iota(jnp.int32, (row_count, row_count), 1)
    moved = (row == (column % frames) * locations + column // frames).astype(F32).astype(BF16)
    by_slot[...] = dot_over(by_frame[...].astype(BF16), moved, 0, 0).astype(BF16)
    for start in range(0, row_count, LANES):
        chunk = slice(start, start + LANES)
        values_in = layer_norm(by_slot[:, chunk].astype(F32), 0)
        normed[:, chunk] = (values_in * (1.0 + levels[:, 4:5]) + levels[:, 3:4]).astype(BF16)
    arriving[0].wait()
    project(columns, normed, projected)
    attend(projected, attended, gains, 2, None, allowed, head_size)
    arriving[1].wait()
    projected[0:width, :] = jnp.dot(out_rows[...], attended[...], preferred_element_type=F32)
    for start in range(0, row_count, LANES):
        chunk = slice(start, start + LANES)
        updated = by_slot[:, chunk].astype(F32) + levels[:, 5:6] * projected[0:width, chunk]
        normed[:, chunk] = layer_norm(updated, 0).astype(BF16)
    predicted[...] = jnp.dot(w_final[...], normed[...], preferred_element_type=F32)


def projection_scratch(rows, width):
    return [
        pltpu.VMEM((3 * width, width), BF16),
        pltpu.VMEM((width, rows), BF16),
        pltpu.VMEM((3 * width, rows), F32),
    ]


def body(
    tokens,
    modulation,
    w_qkv_s,
    w_out_s,
    w_qkv_t,
    w_out_t,
    w_final,
    norm_gains,
    clip_tokens,
    block_clip,
):
    rows, width = tokens.shape[1:]
    head_size = norm_gains.shape[1]
    frames = block_clip.shape[0]
    seq = lax.axis_size("seq")
    locations = rows // seq
    position = lax.axis_index("seq")
    branch_index = lax.axis_index("cfg")
    levels = modulation.transpose(1, 0, 2)
    member = block_clip[:, None] == jnp.arange(clip_tokens.shape[0], dtype=jnp.int32)[None, :]
    lengths = jnp.sum(jnp.where(member, clip_tokens[None, :], 0), axis=1)
    gains = norm_gains.T
    slot_of = jnp.arange(rows // PIECES, dtype=jnp.int32) // frames
    clip_of = jnp.tile(block_clip, rows // PIECES // frames)
    allowed = ((slot_of[:, None] == slot_of[None, :]) & (clip_of[:, None] == clip_of[None, :])).astype(F32)

    first_rows = jnp.pad(w_qkv_s.T, ((0, -w_qkv_s.shape[1] % 8), (0, 0)))
    later_rows = jnp.concatenate([w_qkv_t.T, w_out_t.T, w_out_s.T], axis=0)
    later_rows = jnp.pad(later_rows, ((0, -later_rows.shape[0] % 32), (0, 0)))
    gathered = lax.all_gather(later_rows, ("seq", "cfg"), axis=0, tiled=False)
    shards = gathered.shape[0]
    row_parts, ring_parts = spread_in_plane(first_rows, branch_index)
    params = pltpu.CompilerParams(vmem_limit_bytes=58 * 2**20)
    vmem = pl.BlockSpec(memory_space=pltpu.VMEM)
    smem = pl.BlockSpec(memory_space=pltpu.SMEM)
    anywhere = pl.BlockSpec(memory_space=pl.ANY)
    tile_rows = locations * width // LANES
    cost = pl.CostEstimate(flops=20_000_000_000, bytes_accessed=20_000_000, transcendentals=0)
    attended = pl.pallas_call(
        functools.partial(spatial_kernel, head_size),
        out_shape=jax.ShapeDtypeStruct((width, rows), BF16),
        in_specs=[smem, smem, vmem, vmem, vmem] + [anywhere] * 14,
        out_specs=vmem,
        scratch_shapes=[pltpu.VMEM((shards,) + first_rows.shape, BF16)]
        + projection_scratch(rows, width)
        + [pltpu.SemaphoreType.DMA],
        compiler_params=params,
        cost_estimate=cost,
        name="spatial",
    )(clip_tokens, block_clip, tokens[0], levels, gains, *row_parts, *ring_parts)
    size = rows // PIECES
    residuals = pl.pallas_call(
        functools.partial(mixing_kernel, head_size),
        out_shape=[jax.ShapeDtypeStruct((seq, tile_rows // PIECES, LANES), BF16)] * PIECES,
        in_specs=[vmem, vmem, vmem, anywhere],
        out_specs=[vmem] * PIECES,
        scratch_shapes=[
            pltpu.VMEM((shards, 32, width), BF16),
            pltpu.VMEM((width, width), BF16),
            pltpu.SemaphoreType.DMA,
        ],
        compiler_params=params,
        cost_estimate=cost,
        name="mixing",
    )(tokens[0], levels, attended, gathered)
    held = pl.pallas_call(
        functools.partial(prepare_kernel, head_size),
        out_shape=[
            jax.ShapeDtypeStruct((3 * width, width), BF16),
            jax.ShapeDtypeStruct((width, width), BF16),
        ],
        in_specs=[anywhere],
        out_specs=[vmem] * 2,
        scratch_shapes=[pltpu.VMEM((shards, 80, width), BF16), pltpu.SemaphoreType.DMA],
        compiler_params=params,
        cost_estimate=pl.CostEstimate(flops=0, bytes_accessed=30_000_000, transcendentals=0),
        name="prepare",
    )(gathered)
    found = []
    for residual in residuals:
        received = lax.all_to_all(residual, "seq", split_axis=0, concat_axis=0, tiled=True)
        found.append(
            pl.pallas_call(
                functools.partial(temporal_kernel, head_size),
                out_shape=jax.ShapeDtypeStruct((w_final.shape[1], size), F32),
                in_specs=[vmem] * 5 + [anywhere] * 2,
                out_specs=vmem,
                scratch_shapes=projection_scratch(size, width)
                + [
                    pltpu.VMEM((width, width), BF16),
                    pltpu.VMEM((width, size), BF16),
                    pltpu.VMEM((size, width), F32),
                    pltpu.VMEM((width, size), BF16),
                    pltpu.SemaphoreType.DMA((2,)),
                ],
                compiler_params=params,
                cost_estimate=cost,
                name="temporal",
            )(received, modulation[0].T, gains, allowed, w_final.T, *held)
        )
    predicted = jnp.concatenate(found, axis=1)

    half = predicted.shape[0] // 2
    outgoing = lax.dynamic_slice_in_dim(predicted, (1 - branch_index) * half, half, 0)
    other = lax.ppermute(outgoing, "cfg", [(0, 1), (1, 0)])
    own_part = lax.dynamic_slice_in_dim(predicted, branch_index * half, half, 0)
    conditional = jnp.where(branch_index == 0, own_part, other)
    unconditional = jnp.where(branch_index == 0, other, own_part)
    guided = (unconditional + 7.0 * (conditional - unconditional)).reshape(half, locations, frames)
    location_ids = position * locations + jnp.arange(locations, dtype=jnp.int32)
    inside = location_ids[:, None] < lengths[None, :]
    return jnp.where(inside[None], guided, 0.0).transpose(2, 1, 0)


def solution(mesh):
    in_specs = (
        P(("rep", "seq"), None, None),
        P("cfg", None, None),
        P(None, ("seq", "cfg")),
        P(None, ("seq", "cfg")),
        P(None, ("seq", "cfg")),
        P(None, ("seq", "cfg")),
        P(),
        P(),
        P("rep"),
        P("rep"),
    )
    out_specs = P("rep", "seq", "cfg")
    return jax.shard_map(body, mesh=mesh, in_specs=in_specs, out_specs=out_specs, check_vma=False)
```

```python
import functools
import math

import jax
import jax.numpy as jnp
from jax import lax
from jax.experimental import pallas as pl
from jax.experimental.pallas import tpu as pltpu
from jax.sharding import PartitionSpec as P

BF16 = jnp.bfloat16
F32 = jnp.float32
LANES = 128
TEMPORAL_ROWS = 256
X_RING, Z_RING, SPLIT = 4, 8, 384
X_SLOTS = (0, -1, 1, 2)
Z_SLOTS = (0, -1, -2, -3, 1, 2, 3, 4)

def swap_cores(array):
    return lax.ppermute(array, "cfg", [(0, 1), (1, 0)])


def plane_step(array, along_x, far=1):
    pairs = []
    for x in range(X_RING):
        for z in range(Z_RING):
            for core in range(2):
                by = (1 - 2 * core) * far
                to = ((x + by) % X_RING, z) if along_x else (x, (z + by) % Z_RING)
                pairs.append((2 * (x * Z_RING + z) + core, 2 * (to[0] * Z_RING + to[1]) + core))
    return lax.ppermute(array, ("seq", "cfg"), pairs)


def in_core_order(core, first, second):
    return jnp.where(core == 0, first, second), jnp.where(core == 0, second, first)


def spread_in_plane(own, core):
    pair = jnp.stack(in_core_order(core, own, swap_cores(own)))
    first, second = pair[:, :, :SPLIT], pair[:, :, SPLIT:]

    def own_half(parts):
        return lax.dynamic_index_in_dim(parts, core, 0, keepdims=True)

    near = [plane_step(second, False, far) for far in (1, 2, 3)]
    near.append(plane_step(own_half(second), False, 4))
    mine = jnp.concatenate([plane_step(first, True), plane_step(own_half(first), True, 2)])
    started = jnp.concatenate([mine[:1], mine[2:]], axis=2)
    theirs = swap_cores(mine)
    low, high = in_core_order(core, mine[:2], theirs[:2])
    opposite = jnp.concatenate(in_core_order(core, mine[2:], theirs[2:]))
    row = jnp.stack([first, low, high, opposite])
    rows = [row]
    for _ in range(3):
        rows.append(plane_step(rows[-1], False))
    mine = jnp.concatenate(near) + started * jnp.zeros((), BF16)
    theirs = swap_cores(mine)
    low, high = in_core_order(core, mine[:6], theirs[:6])
    opposite = jnp.concatenate(in_core_order(core, mine[6:], theirs[6:]))
    ring = jnp.concatenate([second, low, high, opposite]).reshape((Z_RING,) + second.shape)
    across = plane_step(ring, True)
    second_step = jnp.concatenate([rows[2]] * 2, axis=3) * jnp.zeros((), BF16)
    beyond = plane_step(lax.dynamic_slice_in_dim(across, 4 * core, 4, 0) + second_step, True)
    rows.append(plane_step(lax.dynamic_slice_in_dim(rows[3], 2 * core, 2, 0), False))
    last_step = jnp.concatenate([jnp.concatenate([rows[4]] * 2, axis=3)] * 2) * jnp.zeros((), BF16)
    rows += [swap_cores(part) for part in rows[1:]]
    return rows, [ring, across, beyond, swap_cores(across), swap_cores(beyond + last_step)]


def pick(table, index):
    found = table[-1]
    for i in range(len(table) - 1):
        found = jnp.where(index == i, table[i], found)
    return found


def plane_copies(rows, rings, landing, sem):
    position, core = lax.axis_index("seq"), lax.axis_index("cfg")
    x, z = position // Z_RING, position % Z_RING
    sign = 1 - 2 * core
    rest = landing.shape[2] - SPLIT
    copies = []

    def to_landing(part, dx, dz, columns):
        shard = 2 * (lax.rem(x + dx + X_RING, X_RING) * Z_RING + lax.rem(z + dz + Z_RING, Z_RING))
        copies.append(pltpu.make_async_copy(part, landing.at[pl.ds(shard, 2), :, columns], sem))

    for k in range(9):
        hop = k if k < 5 else k - 4
        dz = -sign * hop if k < 5 else sign * hop
        for j in range(rows[k].shape[0]):
            dx = X_SLOTS[j] if hop < 4 else pick(X_SLOTS, (2 * core if k < 5 else 2 - 2 * core) + j)
            to_landing(rows[k].at[j], dx, dz, pl.ds(0, SPLIT))
    for part, dx, start in zip(rings, (0, -sign, 2, sign, 2), (0, 0, 4 * core, 0, 4 - 4 * core)):
        for j in range(part.shape[0]):
            dz = Z_SLOTS[j] if part.shape[0] == Z_RING else pick(Z_SLOTS, start + j)
            to_landing(part.at[j], dx, dz, pl.ds(SPLIT, rest))
    return copies


def dot_over(left, right, left_dim, right_dim):
    return lax.dot_general(
        left, right, (((left_dim,), (right_dim,)), ((), ())), preferred_element_type=F32
    )


def layer_norm(values_in, axis):
    average = jnp.mean(values_in, axis=axis, keepdims=True)
    centred = values_in - average
    variance = jnp.mean(centred * centred, axis=axis, keepdims=True)
    return centred * lax.rsqrt(variance + 1e-06)


def lay_out(landing, target, first, count):
    size = 8 * count

    def group(g, carry):
        rows = [landing[8 * g + i][first : first + count] for i in range(8)]
        target[pl.ds(pl.multiple_of(g * size, 16), size), :] = jnp.concatenate(rows, axis=0)
        return carry

    lax.fori_loop(0, landing.shape[0] // 8, group, 0)


def project(columns, normed, projected):
    width = normed.shape[0]

    def kind(i, carry):
        rows = pl.ds(pl.multiple_of(i * width, 16), width)
        projected[rows, :] = jnp.dot(columns[rows, :], normed[...], preferred_element_type=F32)
        return carry

    lax.fori_loop(0, 3, kind, 0)


def unit_heads(head, gain_column):
    total = jnp.sum(head * head, axis=0, keepdims=True)
    return (head * lax.rsqrt(total / head.shape[0] + 1e-06) * gain_column).astype(BF16)


def attend(projected, attended, gains, first_gain, inside, allowed, head_size):
    width = attended.shape[0]
    row_count = attended.shape[1]
    block = row_count if allowed is None else allowed.shape[0]
    factor = math.log2(math.e) / math.sqrt(head_size)
    query_gain = gains[:, first_gain : first_gain + 1] * factor
    key_gain = gains[:, first_gain + 1 : first_gain + 2]
    ones = jnp.ones((1, row_count), F32)
    blank = jnp.zeros((7, row_count), F32)

    def head(h):
        def part(kind):
            return projected[pl.ds(pl.multiple_of(kind * width + h * head_size, 8), head_size), :]

        query = unit_heads(part(0), query_gain)
        key = unit_heads(part(1), key_gain)
        value = jnp.concatenate([part(2), ones, blank], axis=0)
        if inside is not None:
            value = jnp.where(inside, value, 0.0)
        value = value.astype(BF16)
        found = []
        for start in range(0, row_count, block):
            tokens = slice(start, start + block)
            unnormed = jnp.exp2(dot_over(key[:, tokens], query[:, tokens], 0, 0))
            if allowed is not None:
                unnormed = unnormed * allowed[...]
            summed = jnp.dot(value[:, tokens], unnormed.astype(BF16), preferred_element_type=F32)
            found.append(summed[:head_size] / summed[head_size : head_size + 1])
        return jnp.concatenate(found, axis=1) if len(found) > 1 else found[0]

    def pair(p, carry):
        both = jnp.concatenate([head(2 * p), head(2 * p + 1)], axis=0)
        rows = pl.ds(pl.multiple_of(2 * head_size * p, 16), 2 * head_size)
        attended[rows, :] = both.astype(BF16)
        return carry

    lax.fori_loop(0, width // (2 * head_size), pair, 0)


def spatial_kernel(head_size, clip_tokens, block_clip, tokens, levels, gains, *refs):
    rows, rings = refs[:9], refs[9:14]
    attended, landing, columns, normed, projected, sem = refs[14:]
    arriving = plane_copies(rows, rings, landing, sem)
    for copy in arriving:
        copy.start()
    row_count = tokens.shape[0]
    for start in range(0, row_count, LANES):
        chunk = slice(start, start + LANES)
        values_in = layer_norm(tokens[chunk, :].astype(F32), 1) * (1.0 + levels[1]) + levels[0]
        normed[:, chunk] = values_in.astype(BF16).T
    for copy in arriving:
        copy.wait()
    lay_out(landing, columns, 0, 3 * head_size // 4)
    project(columns, normed, projected)
    length = clip_tokens[block_clip[lax.axis_index("seq")]]
    inside = lax.broadcasted_iota(jnp.int32, (head_size + 8, row_count), 1) < length
    attend(projected, attended, gains, 0, inside, None, head_size)


def mixing_kernel(head_size, tokens, levels, attended, gathered, residual, landing, out_rows, sem):
    first, kept = landing.shape[1] * 2, landing.shape[1]
    arriving = pltpu.make_async_copy(gathered.at[:, pl.ds(first, kept), :], landing, sem)
    arriving.start()
    arriving.wait()
    lay_out(landing, out_rows, head_size - first, head_size // 4)
    for start in range(0, tokens.shape[0], 256):
        chunk = slice(start, start + 256)
        projection = dot_over(attended[:, chunk], out_rows[...], 0, 1)
        updated = (tokens[chunk, :].astype(F32) + levels[2] * projection).astype(BF16)
        for d in range(16):
            for j in range(residual.shape[1] // 16):
                residual[start // 16 + d, 16 * j : 16 * j + 16, :] = updated[
                    16 * d : 16 * d + 16, LANES * j : LANES * (j + 1)
                ]


def prepare_kernel(head_size, gathered, columns, out_rows, landing, sem):
    arriving = pltpu.make_async_copy(gathered.at[:, pl.ds(0, landing.shape[1]), :], landing, sem)
    arriving.start()
    arriving.wait()
    share = 3 * head_size // 4
    lay_out(landing, columns, 0, share)
    lay_out(landing, out_rows, share, head_size // 4)


def temporal_kernel(head_size, received, levels, gains, allowed, w_final, held_columns, held_rows, predicted,
                    columns, normed, projected, out_rows, attended, by_frame, by_slot, sems):
    arriving = [
        pltpu.make_async_copy(held_columns, columns, sems.at[0]),
        pltpu.make_async_copy(held_rows, out_rows, sems.at[1]),
    ]
    for copy in arriving:
        copy.start()
    frames = received.shape[0]
    width, row_count = normed.shape
    locations = row_count // frames

    def unpack(b, carry):
        rows = pl.ds(pl.multiple_of(b * locations, 16), locations)
        for j in range(width // LANES):
            by_frame[rows, LANES * j : LANES * (j + 1)] = received[b, 16 * j : 16 * j + 16, :]
        return carry

    lax.fori_loop(0, frames, unpack, 0)
    row = lax.broadcasted_iota(jnp.int32, (row_count, row_count), 0)
    column = lax.broadcasted_iota(jnp.int32, (row_count, row_count), 1)
    moved = (row == (column % frames) * locations + column // frames).astype(F32).astype(BF16)
    by_slot[...] = dot_over(by_frame[...], moved, 0, 0).astype(BF16)
    for start in range(0, row_count, LANES):
        chunk = slice(start, start + LANES)
        values_in = layer_norm(by_slot[:, chunk].astype(F32), 0)
        normed[:, chunk] = (values_in * (1.0 + levels[:, 4:5]) + levels[:, 3:4]).astype(BF16)
    arriving[0].wait()
    project(columns, normed, projected)
    attend(projected, attended, gains, 2, None, allowed, head_size)
    arriving[1].wait()
    projected[0:width, :] = jnp.dot(out_rows[...], attended[...], preferred_element_type=F32)
    for start in range(0, row_count, LANES):
        chunk = slice(start, start + LANES)
        updated = by_slot[:, chunk].astype(F32) + levels[:, 5:6] * projected[0:width, chunk]
        normed[:, chunk] = layer_norm(updated, 0).astype(BF16)
    predicted[...] = jnp.dot(w_final[...], normed[...], preferred_element_type=F32)


def projection_scratch(rows, width):
    return [
        pltpu.VMEM((3 * width, width), BF16),
        pltpu.VMEM((width, rows), BF16),
        pltpu.VMEM((3 * width, rows), F32),
    ]


def body(
    tokens,
    modulation,
    w_qkv_s,
    w_out_s,
    w_qkv_t,
    w_out_t,
    w_final,
    norm_gains,
    clip_tokens,
    block_clip,
):
    rows, width = tokens.shape[1:]
    head_size = norm_gains.shape[1]
    frames = block_clip.shape[0]
    seq = lax.axis_size("seq")
    locations = rows // seq
    position = lax.axis_index("seq")
    branch_index = lax.axis_index("cfg")
    levels = modulation.transpose(1, 0, 2)
    member = block_clip[:, None] == jnp.arange(clip_tokens.shape[0], dtype=jnp.int32)[None, :]
    lengths = jnp.sum(jnp.where(member, clip_tokens[None, :], 0), axis=1)
    gains = norm_gains.T
    slot_of = jnp.arange(TEMPORAL_ROWS, dtype=jnp.int32) // frames
    clip_of = jnp.tile(block_clip, TEMPORAL_ROWS // frames)
    allowed = ((slot_of[:, None] == slot_of[None, :]) & (clip_of[:, None] == clip_of[None, :])).astype(F32)

    first_rows = jnp.pad(w_qkv_s.T, ((0, -w_qkv_s.shape[1] % 8), (0, 0)))
    later_rows = jnp.concatenate([w_qkv_t.T, w_out_t.T, w_out_s.T], axis=0)
    later_rows = jnp.pad(later_rows, ((0, -later_rows.shape[0] % 32), (0, 0)))
    gathered = lax.all_gather(later_rows, ("seq", "cfg"), axis=0, tiled=False)
    shards = gathered.shape[0]
    row_parts, ring_parts = spread_in_plane(first_rows, branch_index)
    params = pltpu.CompilerParams(vmem_limit_bytes=58 * 2**20)
    vmem = pl.BlockSpec(memory_space=pltpu.VMEM)
    smem = pl.BlockSpec(memory_space=pltpu.SMEM)
    anywhere = pl.BlockSpec(memory_space=pl.ANY)
    tile_rows = locations * width // LANES
    cost = pl.CostEstimate(flops=20_000_000_000, bytes_accessed=20_000_000, transcendentals=0)
    attended = pl.pallas_call(
        functools.partial(spatial_kernel, head_size),
        out_shape=jax.ShapeDtypeStruct((width, rows), BF16),
        in_specs=[smem, smem, vmem, vmem, vmem] + [anywhere] * 14,
        out_specs=vmem,
        scratch_shapes=[pltpu.VMEM((shards,) + first_rows.shape, BF16)]
        + projection_scratch(rows, width)
        + [pltpu.SemaphoreType.DMA],
        compiler_params=params,
        cost_estimate=cost,
        name="spatial",
    )(clip_tokens, block_clip, tokens[0], levels, gains, *row_parts, *ring_parts)
    residual = pl.pallas_call(
        functools.partial(mixing_kernel, head_size),
        out_shape=jax.ShapeDtypeStruct((seq, tile_rows, LANES), BF16),
        in_specs=[vmem, vmem, vmem, anywhere],
        out_specs=vmem,
        scratch_shapes=[
            pltpu.VMEM((shards, 32, width), BF16),
            pltpu.VMEM((width, width), BF16),
            pltpu.SemaphoreType.DMA,
        ],
        compiler_params=params,
        cost_estimate=cost,
        name="mixing",
    )(tokens[0], levels, attended, gathered)
    received = lax.all_to_all(residual, "seq", split_axis=0, concat_axis=0, tiled=True)
    held = pl.pallas_call(
        functools.partial(prepare_kernel, head_size),
        out_shape=[
            jax.ShapeDtypeStruct((3 * width, width), BF16),
            jax.ShapeDtypeStruct((width, width), BF16),
        ],
        in_specs=[anywhere],
        out_specs=[vmem] * 2,
        scratch_shapes=[pltpu.VMEM((shards, 80, width), BF16), pltpu.SemaphoreType.DMA],
        compiler_params=params,
        cost_estimate=pl.CostEstimate(flops=0, bytes_accessed=30_000_000, transcendentals=0),
        name="prepare",
    )(gathered)
    predicted = pl.pallas_call(
        functools.partial(temporal_kernel, head_size),
        out_shape=jax.ShapeDtypeStruct((w_final.shape[1], rows), F32),
        in_specs=[vmem] * 5 + [anywhere] * 2,
        out_specs=vmem,
        scratch_shapes=projection_scratch(rows, width)
        + [
            pltpu.VMEM((width, width), BF16),
            pltpu.VMEM((width, rows), BF16),
            pltpu.VMEM((rows, width), BF16),
            pltpu.VMEM((width, rows), BF16),
            pltpu.SemaphoreType.DMA((2,)),
        ],
        compiler_params=params,
        cost_estimate=cost,
        name="temporal",
    )(received, modulation[0].T, gains, allowed, w_final.T, *held)

    half = predicted.shape[0] // 2
    outgoing = lax.dynamic_slice_in_dim(predicted, (1 - branch_index) * half, half, 0)
    other = lax.ppermute(outgoing, "cfg", [(0, 1), (1, 0)])
    own_part = lax.dynamic_slice_in_dim(predicted, branch_index * half, half, 0)
    conditional = jnp.where(branch_index == 0, own_part, other)
    unconditional = jnp.where(branch_index == 0, other, own_part)
    guided = (unconditional + 7.0 * (conditional - unconditional)).reshape(half, locations, frames)
    location_ids = position * locations + jnp.arange(locations, dtype=jnp.int32)
    inside = location_ids[:, None] < lengths[None, :]
    return jnp.where(inside[None], guided, 0.0).transpose(2, 1, 0)


def solution(mesh):
    in_specs = (
        P(("rep", "seq"), None, None),
        P("cfg", None, None),
        P(None, ("seq", "cfg")),
        P(None, ("seq", "cfg")),
        P(None, ("seq", "cfg")),
        P(None, ("seq", "cfg")),
        P(),
        P(),
        P("rep"),
        P("rep"),
    )
    out_specs = P("rep", "seq", "cfg")
    return jax.shard_map(body, mesh=mesh, in_specs=in_specs, out_specs=out_specs, check_vma=False)
```

```python
import functools
import math

import jax
import jax.numpy as jnp
from jax import lax
from jax.experimental import pallas as pl
from jax.experimental.pallas import tpu as pltpu
from jax.sharding import PartitionSpec as P

BF16 = jnp.bfloat16
F32 = jnp.float32
LANES = 128
TEMPORAL_ROWS = 256
X_RING, Z_RING, SPLIT = 4, 8, 512
X_SLOTS = (0, -1, 1, 2)
Z_SLOTS = (0, -1, -2, -3, 1, 2, 3, 4)

def swap_cores(array):
    return lax.ppermute(array, "cfg", [(0, 1), (1, 0)])


def plane_step(array, along_x, far=1):
    pairs = []
    for x in range(X_RING):
        for z in range(Z_RING):
            for core in range(2):
                by = (1 - 2 * core) * far
                to = ((x + by) % X_RING, z) if along_x else (x, (z + by) % Z_RING)
                pairs.append((2 * (x * Z_RING + z) + core, 2 * (to[0] * Z_RING + to[1]) + core))
    return lax.ppermute(array, ("seq", "cfg"), pairs)


def in_core_order(core, first, second):
    return jnp.where(core == 0, first, second), jnp.where(core == 0, second, first)


def spread_in_plane(own, core):
    pair = jnp.stack(in_core_order(core, own, swap_cores(own)))
    first, second = pair[:, :, :SPLIT], pair[:, :, SPLIT:]

    def own_half(parts):
        return lax.dynamic_index_in_dim(parts, core, 0, keepdims=True)

    near = [plane_step(second, False, far) for far in (1, 2, 3)]
    near.append(plane_step(own_half(second), False, 4))
    mine = jnp.concatenate([plane_step(first, True), plane_step(own_half(first), True, 2)])
    theirs = swap_cores(mine)
    low, high = in_core_order(core, mine[:2], theirs[:2])
    opposite = jnp.concatenate(in_core_order(core, mine[2:], theirs[2:]))
    row = jnp.stack([first, low, high, opposite])
    rows = [row]
    for _ in range(3):
        rows.append(plane_step(rows[-1], False))
    mine = jnp.concatenate(near)
    theirs = swap_cores(mine)
    low, high = in_core_order(core, mine[:6], theirs[:6])
    opposite = jnp.concatenate(in_core_order(core, mine[6:], theirs[6:]))
    ring = jnp.concatenate([second, low, high, opposite]).reshape((Z_RING,) + second.shape)
    across = plane_step(ring, True)
    beyond = plane_step(lax.dynamic_slice_in_dim(across, 4 * core, 4, 0), True)
    rows.append(plane_step(lax.dynamic_slice_in_dim(rows[3], 2 * core, 2, 0), False))
    rows += [swap_cores(part) for part in rows[1:]]
    return rows, [ring, across, beyond, swap_cores(across), swap_cores(beyond)]


def pick(table, index):
    found = table[-1]
    for i in range(len(table) - 1):
        found = jnp.where(index == i, table[i], found)
    return found


def plane_copies(rows, rings, landing, sem):
    position, core = lax.axis_index("seq"), lax.axis_index("cfg")
    x, z = position // Z_RING, position % Z_RING
    sign = 1 - 2 * core
    rest = landing.shape[2] - SPLIT
    copies = []

    def to_landing(part, dx, dz, columns):
        shard = 2 * (lax.rem(x + dx + X_RING, X_RING) * Z_RING + lax.rem(z + dz + Z_RING, Z_RING))
        copies.append(pltpu.make_async_copy(part, landing.at[pl.ds(shard, 2), :, columns], sem))

    for k in range(9):
        hop = k if k < 5 else k - 4
        dz = -sign * hop if k < 5 else sign * hop
        for j in range(rows[k].shape[0]):
            dx = X_SLOTS[j] if hop < 4 else pick(X_SLOTS, (2 * core if k < 5 else 2 - 2 * core) + j)
            to_landing(rows[k].at[j], dx, dz, pl.ds(0, SPLIT))
    for part, dx, start in zip(rings, (0, -sign, 2, sign, 2), (0, 0, 4 * core, 0, 4 - 4 * core)):
        for j in range(part.shape[0]):
            dz = Z_SLOTS[j] if part.shape[0] == Z_RING else pick(Z_SLOTS, start + j)
            to_landing(part.at[j], dx, dz, pl.ds(SPLIT, rest))
    return copies


def dot_over(left, right, left_dim, right_dim):
    return lax.dot_general(
        left, right, (((left_dim,), (right_dim,)), ((), ())), preferred_element_type=F32
    )


def layer_norm(values_in, axis):
    average = jnp.mean(values_in, axis=axis, keepdims=True)
    centred = values_in - average
    variance = jnp.mean(centred * centred, axis=axis, keepdims=True)
    return centred * lax.rsqrt(variance + 1e-06)


def lay_out(landing, target, first, count):
    size = 8 * count

    def group(g, carry):
        rows = [landing[8 * g + i][first : first + count] for i in range(8)]
        target[pl.ds(pl.multiple_of(g * size, 16), size), :] = jnp.concatenate(rows, axis=0)
        return carry

    lax.fori_loop(0, landing.shape[0] // 8, group, 0)


def project(columns, normed, projected):
    width = normed.shape[0]

    def kind(i, carry):
        rows = pl.ds(pl.multiple_of(i * width, 16), width)
        projected[rows, :] = jnp.dot(columns[rows, :], normed[...], preferred_element_type=F32)
        return carry

    lax.fori_loop(0, 3, kind, 0)


def unit_heads(head, gain_column):
    total = jnp.sum(head * head, axis=0, keepdims=True)
    return (head * lax.rsqrt(total / head.shape[0] + 1e-06) * gain_column).astype(BF16)


def attend(projected, attended, gains, first_gain, inside, allowed, head_size):
    width = attended.shape[0]
    row_count = attended.shape[1]
    block = row_count if allowed is None else allowed.shape[0]
    factor = math.log2(math.e) / math.sqrt(head_size)
    query_gain = gains[:, first_gain : first_gain + 1] * factor
    key_gain = gains[:, first_gain + 1 : first_gain + 2]
    ones = jnp.ones((1, row_count), F32)
    blank = jnp.zeros((7, row_count), F32)

    def head(h):
        def part(kind):
            return projected[pl.ds(pl.multiple_of(kind * width + h * head_size, 8), head_size), :]

        query = unit_heads(part(0), query_gain)
        key = unit_heads(part(1), key_gain)
        value = jnp.concatenate([part(2), ones, blank], axis=0)
        if inside is not None:
            value = jnp.where(inside, value, 0.0)
        value = value.astype(BF16)
        found = []
        for start in range(0, row_count, block):
            tokens = slice(start, start + block)
            unnormed = jnp.exp2(dot_over(key[:, tokens], query[:, tokens], 0, 0))
            if allowed is not None:
                unnormed = unnormed * allowed[...]
            summed = jnp.dot(value[:, tokens], unnormed.astype(BF16), preferred_element_type=F32)
            found.append(summed[:head_size] / summed[head_size : head_size + 1])
        return jnp.concatenate(found, axis=1) if len(found) > 1 else found[0]

    def pair(p, carry):
        both = jnp.concatenate([head(2 * p), head(2 * p + 1)], axis=0)
        rows = pl.ds(pl.multiple_of(2 * head_size * p, 16), 2 * head_size)
        attended[rows, :] = both.astype(BF16)
        return carry

    lax.fori_loop(0, width // (2 * head_size), pair, 0)


def spatial_kernel(head_size, clip_tokens, block_clip, tokens, levels, gains, *refs):
    rows, rings = refs[:9], refs[9:14]
    attended, landing, columns, normed, projected, sem = refs[14:]
    arriving = plane_copies(rows, rings, landing, sem)
    for copy in arriving:
        copy.start()
    row_count = tokens.shape[0]
    for start in range(0, row_count, LANES):
        chunk = slice(start, start + LANES)
        values_in = layer_norm(tokens[chunk, :].astype(F32), 1) * (1.0 + levels[1]) + levels[0]
        normed[:, chunk] = values_in.astype(BF16).T
    for copy in arriving:
        copy.wait()
    lay_out(landing, columns, 0, 3 * head_size // 4)
    project(columns, normed, projected)
    length = clip_tokens[block_clip[lax.axis_index("seq")]]
    inside = lax.broadcasted_iota(jnp.int32, (head_size + 8, row_count), 1) < length
    attend(projected, attended, gains, 0, inside, None, head_size)


def mixing_kernel(head_size, tokens, levels, attended, gathered, residual, landing, out_rows, sem):
    first, kept = landing.shape[1] * 2, landing.shape[1]
    arriving = pltpu.make_async_copy(gathered.at[:, pl.ds(first, kept), :], landing, sem)
    arriving.start()
    arriving.wait()
    lay_out(landing, out_rows, head_size - first, head_size // 4)
    for start in range(0, tokens.shape[0], 256):
        chunk = slice(start, start + 256)
        projection = dot_over(attended[:, chunk], out_rows[...], 0, 1)
        updated = (tokens[chunk, :].astype(F32) + levels[2] * projection).astype(BF16)
        for d in range(16):
            for j in range(residual.shape[1] // 16):
                residual[start // 16 + d, 16 * j : 16 * j + 16, :] = updated[
                    16 * d : 16 * d + 16, LANES * j : LANES * (j + 1)
                ]


def prepare_kernel(head_size, gathered, columns, out_rows, landing, sem):
    arriving = pltpu.make_async_copy(gathered.at[:, pl.ds(0, landing.shape[1]), :], landing, sem)
    arriving.start()
    arriving.wait()
    share = 3 * head_size // 4
    lay_out(landing, columns, 0, share)
    lay_out(landing, out_rows, share, head_size // 4)


def temporal_kernel(head_size, received, levels, gains, allowed, w_final, held_columns, held_rows, predicted,
                    columns, normed, projected, out_rows, attended, by_frame, by_slot, sems):
    arriving = [
        pltpu.make_async_copy(held_columns, columns, sems.at[0]),
        pltpu.make_async_copy(held_rows, out_rows, sems.at[1]),
    ]
    for copy in arriving:
        copy.start()
    frames = received.shape[0]
    width, row_count = normed.shape
    locations = row_count // frames

    def unpack(b, carry):
        rows = pl.ds(pl.multiple_of(b * locations, 16), locations)
        for j in range(width // LANES):
            by_frame[rows, LANES * j : LANES * (j + 1)] = received[b, 16 * j : 16 * j + 16, :]
        return carry

    lax.fori_loop(0, frames, unpack, 0)
    row = lax.broadcasted_iota(jnp.int32, (row_count, row_count), 0)
    column = lax.broadcasted_iota(jnp.int32, (row_count, row_count), 1)
    moved = (row == (column % frames) * locations + column // frames).astype(F32).astype(BF16)
    by_slot[...] = dot_over(by_frame[...], moved, 0, 0).astype(BF16)
    for start in range(0, row_count, LANES):
        chunk = slice(start, start + LANES)
        values_in = layer_norm(by_slot[:, chunk].astype(F32), 0)
        normed[:, chunk] = (values_in * (1.0 + levels[:, 4:5]) + levels[:, 3:4]).astype(BF16)
    arriving[0].wait()
    project(columns, normed, projected)
    attend(projected, attended, gains, 2, None, allowed, head_size)
    arriving[1].wait()
    projected[0:width, :] = jnp.dot(out_rows[...], attended[...], preferred_element_type=F32)
    for start in range(0, row_count, LANES):
        chunk = slice(start, start + LANES)
        updated = by_slot[:, chunk].astype(F32) + levels[:, 5:6] * projected[0:width, chunk]
        normed[:, chunk] = layer_norm(updated, 0).astype(BF16)
    predicted[...] = jnp.dot(w_final[...], normed[...], preferred_element_type=F32)


def projection_scratch(rows, width):
    return [
        pltpu.VMEM((3 * width, width), BF16),
        pltpu.VMEM((width, rows), BF16),
        pltpu.VMEM((3 * width, rows), F32),
    ]


def body(
    tokens,
    modulation,
    w_qkv_s,
    w_out_s,
    w_qkv_t,
    w_out_t,
    w_final,
    norm_gains,
    clip_tokens,
    block_clip,
):
    rows, width = tokens.shape[1:]
    head_size = norm_gains.shape[1]
    frames = block_clip.shape[0]
    seq = lax.axis_size("seq")
    locations = rows // seq
    position = lax.axis_index("seq")
    branch_index = lax.axis_index("cfg")
    levels = modulation.transpose(1, 0, 2)
    member = block_clip[:, None] == jnp.arange(clip_tokens.shape[0], dtype=jnp.int32)[None, :]
    lengths = jnp.sum(jnp.where(member, clip_tokens[None, :], 0), axis=1)
    gains = norm_gains.T
    slot_of = jnp.arange(TEMPORAL_ROWS, dtype=jnp.int32) // frames
    clip_of = jnp.tile(block_clip, TEMPORAL_ROWS // frames)
    allowed = ((slot_of[:, None] == slot_of[None, :]) & (clip_of[:, None] == clip_of[None, :])).astype(F32)

    first_rows = jnp.pad(w_qkv_s.T, ((0, -w_qkv_s.shape[1] % 8), (0, 0)))
    later_rows = jnp.concatenate([w_qkv_t.T, w_out_t.T, w_out_s.T], axis=0)
    later_rows = jnp.pad(later_rows, ((0, -later_rows.shape[0] % 32), (0, 0)))
    gathered = lax.all_gather(later_rows, ("seq", "cfg"), axis=0, tiled=False)
    shards = gathered.shape[0]
    row_parts, ring_parts = spread_in_plane(first_rows, branch_index)
    small = pltpu.CompilerParams(vmem_limit_bytes=40 * 2**20)
    params = pltpu.CompilerParams(vmem_limit_bytes=58 * 2**20)
    vmem = pl.BlockSpec(memory_space=pltpu.VMEM)
    smem = pl.BlockSpec(memory_space=pltpu.SMEM)
    anywhere = pl.BlockSpec(memory_space=pl.ANY)
    tile_rows = locations * width // LANES
    cost = pl.CostEstimate(flops=20_000_000_000, bytes_accessed=20_000_000, transcendentals=0)
    attended = pl.pallas_call(
        functools.partial(spatial_kernel, head_size),
        out_shape=jax.ShapeDtypeStruct((width, rows), BF16),
        in_specs=[smem, smem, vmem, vmem, vmem] + [anywhere] * 14,
        out_specs=vmem,
        scratch_shapes=[pltpu.VMEM((shards,) + first_rows.shape, BF16)]
        + projection_scratch(rows, width)
        + [pltpu.SemaphoreType.DMA],
        compiler_params=small,
        cost_estimate=cost,
        name="spatial",
    )(clip_tokens, block_clip, tokens[0], levels, gains, *row_parts, *ring_parts)
    residual = pl.pallas_call(
        functools.partial(mixing_kernel, head_size),
        out_shape=jax.ShapeDtypeStruct((seq, tile_rows, LANES), BF16),
        in_specs=[vmem, vmem, vmem, anywhere],
        out_specs=vmem,
        scratch_shapes=[
            pltpu.VMEM((shards, 32, width), BF16),
            pltpu.VMEM((width, width), BF16),
            pltpu.SemaphoreType.DMA,
        ],
        compiler_params=params,
        cost_estimate=cost,
        name="mixing",
    )(tokens[0], levels, attended, gathered)
    received = lax.all_to_all(residual, "seq", split_axis=0, concat_axis=0, tiled=True)
    held = pl.pallas_call(
        functools.partial(prepare_kernel, head_size),
        out_shape=[
            jax.ShapeDtypeStruct((3 * width, width), BF16),
            jax.ShapeDtypeStruct((width, width), BF16),
        ],
        in_specs=[anywhere],
        out_specs=[vmem] * 2,
        scratch_shapes=[pltpu.VMEM((shards, 80, width), BF16), pltpu.SemaphoreType.DMA],
        compiler_params=params,
        cost_estimate=pl.CostEstimate(flops=0, bytes_accessed=30_000_000, transcendentals=0),
        name="prepare",
    )(gathered)
    predicted = pl.pallas_call(
        functools.partial(temporal_kernel, head_size),
        out_shape=jax.ShapeDtypeStruct((w_final.shape[1], rows), F32),
        in_specs=[vmem] * 5 + [anywhere] * 2,
        out_specs=vmem,
        scratch_shapes=projection_scratch(rows, width)
        + [
            pltpu.VMEM((width, width), BF16),
            pltpu.VMEM((width, rows), BF16),
            pltpu.VMEM((rows, width), BF16),
            pltpu.VMEM((width, rows), BF16),
            pltpu.SemaphoreType.DMA((2,)),
        ],
        compiler_params=params,
        cost_estimate=cost,
        name="temporal",
    )(received, modulation[0].T, gains, allowed, w_final.T, *held)

    half = predicted.shape[0] // 2
    outgoing = lax.dynamic_slice_in_dim(predicted, (1 - branch_index) * half, half, 0)
    other = lax.ppermute(outgoing, "cfg", [(0, 1), (1, 0)])
    own_part = lax.dynamic_slice_in_dim(predicted, branch_index * half, half, 0)
    conditional = jnp.where(branch_index == 0, own_part, other)
    unconditional = jnp.where(branch_index == 0, other, own_part)
    guided = (unconditional + 7.0 * (conditional - unconditional)).reshape(half, locations, frames)
    location_ids = position * locations + jnp.arange(locations, dtype=jnp.int32)
    inside = location_ids[:, None] < lengths[None, :]
    return jnp.where(inside[None], guided, 0.0).transpose(2, 1, 0)


def solution(mesh):
    in_specs = (
        P(("rep", "seq"), None, None),
        P("cfg", None, None),
        P(None, ("seq", "cfg")),
        P(None, ("seq", "cfg")),
        P(None, ("seq", "cfg")),
        P(None, ("seq", "cfg")),
        P(),
        P(),
        P("rep"),
        P("rep"),
    )
    out_specs = P("rep", "seq", "cfg")
    return jax.shard_map(body, mesh=mesh, in_specs=in_specs, out_specs=out_specs, check_vma=False)
```

```python
import functools
import math

import jax
import jax.numpy as jnp
from jax import lax
from jax.experimental import pallas as pl
from jax.experimental.pallas import tpu as pltpu
from jax.sharding import PartitionSpec as P

BF16 = jnp.bfloat16
F32 = jnp.float32
LANES = 128
TEMPORAL_ROWS = 256
X_RING, Z_RING, SPLIT = 4, 8, 512
X_SLOTS = (0, -1, 1, 2)
Z_SLOTS = (0, -1, -2, -3, 1, 2, 3, 4)

def swap_cores(array):
    return lax.ppermute(array, "cfg", [(0, 1), (1, 0)])


def plane_step(array, along_x, far=1):
    pairs = []
    for x in range(X_RING):
        for z in range(Z_RING):
            for core in range(2):
                by = (1 - 2 * core) * far
                to = ((x + by) % X_RING, z) if along_x else (x, (z + by) % Z_RING)
                pairs.append((2 * (x * Z_RING + z) + core, 2 * (to[0] * Z_RING + to[1]) + core))
    return lax.ppermute(array, ("seq", "cfg"), pairs)


def in_core_order(core, first, second):
    return jnp.where(core == 0, first, second), jnp.where(core == 0, second, first)


def spread_in_plane(own, core):
    pair = jnp.stack(in_core_order(core, own, swap_cores(own)))
    first, second = pair[:, :, :SPLIT], pair[:, :, SPLIT:]

    def own_half(parts):
        return lax.dynamic_index_in_dim(parts, core, 0, keepdims=True)

    near = [plane_step(second, False, far) for far in (1, 2, 3)]
    near.append(plane_step(own_half(second), False, 4))
    mine = jnp.concatenate([plane_step(first, True), plane_step(own_half(first), True, 2)])
    theirs = swap_cores(mine)
    low, high = in_core_order(core, mine[:2], theirs[:2])
    opposite = jnp.concatenate(in_core_order(core, mine[2:], theirs[2:]))
    row = jnp.stack([first, low, high, opposite])
    rows = [row]
    for _ in range(3):
        rows.append(plane_step(rows[-1], False))
    mine = jnp.concatenate(near)
    theirs = swap_cores(mine)
    low, high = in_core_order(core, mine[:6], theirs[:6])
    opposite = jnp.concatenate(in_core_order(core, mine[6:], theirs[6:]))
    ring = jnp.concatenate([second, low, high, opposite]).reshape((Z_RING,) + second.shape)
    across = plane_step(ring, True)
    beyond = plane_step(lax.dynamic_slice_in_dim(across, 4 * core, 4, 0), True)
    rows.append(plane_step(lax.dynamic_slice_in_dim(rows[0], 2 * core, 2, 0), False, 4))
    rows += [swap_cores(part) for part in rows[1:]]
    return rows, [ring, across, beyond, swap_cores(across), swap_cores(beyond)]


def pick(table, index):
    found = table[-1]
    for i in range(len(table) - 1):
        found = jnp.where(index == i, table[i], found)
    return found


def plane_copies(rows, rings, landing, sem):
    position, core = lax.axis_index("seq"), lax.axis_index("cfg")
    x, z = position // Z_RING, position % Z_RING
    sign = 1 - 2 * core
    rest = landing.shape[2] - SPLIT
    copies = []

    def to_landing(part, dx, dz, columns):
        shard = 2 * (lax.rem(x + dx + X_RING, X_RING) * Z_RING + lax.rem(z + dz + Z_RING, Z_RING))
        copies.append(pltpu.make_async_copy(part, landing.at[pl.ds(shard, 2), :, columns], sem))

    for k in range(9):
        hop = k if k < 5 else k - 4
        dz = -sign * hop if k < 5 else sign * hop
        for j in range(rows[k].shape[0]):
            dx = X_SLOTS[j] if hop < 4 else pick(X_SLOTS, (2 * core if k < 5 else 2 - 2 * core) + j)
            to_landing(rows[k].at[j], dx, dz, pl.ds(0, SPLIT))
    for part, dx, start in zip(rings, (0, -sign, 2, sign, 2), (0, 0, 4 * core, 0, 4 - 4 * core)):
        for j in range(part.shape[0]):
            dz = Z_SLOTS[j] if part.shape[0] == Z_RING else pick(Z_SLOTS, start + j)
            to_landing(part.at[j], dx, dz, pl.ds(SPLIT, rest))
    return copies


def dot_over(left, right, left_dim, right_dim):
    return lax.dot_general(
        left, right, (((left_dim,), (right_dim,)), ((), ())), preferred_element_type=F32
    )


def layer_norm(values_in, axis):
    average = jnp.mean(values_in, axis=axis, keepdims=True)
    centred = values_in - average
    variance = jnp.mean(centred * centred, axis=axis, keepdims=True)
    return centred * lax.rsqrt(variance + 1e-06)


def lay_out(landing, target, first, count):
    size = 8 * count

    def group(g, carry):
        rows = [landing[8 * g + i][first : first + count] for i in range(8)]
        target[pl.ds(pl.multiple_of(g * size, 16), size), :] = jnp.concatenate(rows, axis=0)
        return carry

    lax.fori_loop(0, landing.shape[0] // 8, group, 0)


def project(columns, normed, projected):
    width = normed.shape[0]

    def kind(i, carry):
        rows = pl.ds(pl.multiple_of(i * width, 16), width)
        projected[rows, :] = jnp.dot(columns[rows, :], normed[...], preferred_element_type=F32)
        return carry

    lax.fori_loop(0, 3, kind, 0)


def unit_heads(head, gain_column):
    total = jnp.sum(head * head, axis=0, keepdims=True)
    return (head * lax.rsqrt(total / head.shape[0] + 1e-06) * gain_column).astype(BF16)


def attend(projected, attended, gains, first_gain, inside, allowed, head_size):
    width = attended.shape[0]
    row_count = attended.shape[1]
    block = row_count if allowed is None else allowed.shape[0]
    factor = math.log2(math.e) / math.sqrt(head_size)
    query_gain = gains[:, first_gain : first_gain + 1] * factor
    key_gain = gains[:, first_gain + 1 : first_gain + 2]
    ones = jnp.ones((1, row_count), F32)
    blank = jnp.zeros((7, row_count), F32)

    def head(h):
        def part(kind):
            return projected[pl.ds(pl.multiple_of(kind * width + h * head_size, 8), head_size), :]

        query = unit_heads(part(0), query_gain)
        key = unit_heads(part(1), key_gain)
        value = jnp.concatenate([part(2), ones, blank], axis=0)
        if inside is not None:
            value = jnp.where(inside, value, 0.0)
        value = value.astype(BF16)
        found = []
        for start in range(0, row_count, block):
            tokens = slice(start, start + block)
            unnormed = jnp.exp2(dot_over(key[:, tokens], query[:, tokens], 0, 0))
            if allowed is not None:
                unnormed = unnormed * allowed[...]
            summed = jnp.dot(value[:, tokens], unnormed.astype(BF16), preferred_element_type=F32)
            found.append(summed[:head_size] / summed[head_size : head_size + 1])
        return jnp.concatenate(found, axis=1) if len(found) > 1 else found[0]

    def pair(p, carry):
        both = jnp.concatenate([head(2 * p), head(2 * p + 1)], axis=0)
        rows = pl.ds(pl.multiple_of(2 * head_size * p, 16), 2 * head_size)
        attended[rows, :] = both.astype(BF16)
        return carry

    lax.fori_loop(0, width // (2 * head_size), pair, 0)


def spatial_kernel(head_size, clip_tokens, block_clip, tokens, levels, gains, *refs):
    rows, rings = refs[:9], refs[9:14]
    attended, landing, columns, normed, projected, sem = refs[14:]
    arriving = plane_copies(rows, rings, landing, sem)
    for copy in arriving:
        copy.start()
    row_count = tokens.shape[0]
    for start in range(0, row_count, LANES):
        chunk = slice(start, start + LANES)
        values_in = layer_norm(tokens[chunk, :].astype(F32), 1) * (1.0 + levels[1]) + levels[0]
        normed[:, chunk] = values_in.astype(BF16).T
    for copy in arriving:
        copy.wait()
    lay_out(landing, columns, 0, 3 * head_size // 4)
    project(columns, normed, projected)
    length = clip_tokens[block_clip[lax.axis_index("seq")]]
    inside = lax.broadcasted_iota(jnp.int32, (head_size + 8, row_count), 1) < length
    attend(projected, attended, gains, 0, inside, None, head_size)


def mixing_kernel(head_size, tokens, levels, attended, gathered, residual, landing, out_rows, sem):
    first, kept = landing.shape[1] * 2, landing.shape[1]
    arriving = pltpu.make_async_copy(gathered.at[:, pl.ds(first, kept), :], landing, sem)
    arriving.start()
    arriving.wait()
    lay_out(landing, out_rows, head_size - first, head_size // 4)
    for start in range(0, tokens.shape[0], 256):
        chunk = slice(start, start + 256)
        projection = dot_over(attended[:, chunk], out_rows[...], 0, 1)
        updated = (tokens[chunk, :].astype(F32) + levels[2] * projection).astype(BF16)
        for d in range(16):
            for j in range(residual.shape[1] // 16):
                residual[start // 16 + d, 16 * j : 16 * j + 16, :] = updated[
                    16 * d : 16 * d + 16, LANES * j : LANES * (j + 1)
                ]


def prepare_kernel(head_size, gathered, columns, out_rows, landing, sem):
    arriving = pltpu.make_async_copy(gathered.at[:, pl.ds(0, landing.shape[1]), :], landing, sem)
    arriving.start()
    arriving.wait()
    share = 3 * head_size // 4
    lay_out(landing, columns, 0, share)
    lay_out(landing, out_rows, share, head_size // 4)


def temporal_kernel(head_size, received, levels, gains, allowed, w_final, held_columns, held_rows, predicted,
                    columns, normed, projected, out_rows, attended, by_frame, by_slot, sems):
    arriving = [
        pltpu.make_async_copy(held_columns, columns, sems.at[0]),
        pltpu.make_async_copy(held_rows, out_rows, sems.at[1]),
    ]
    for copy in arriving:
        copy.start()
    frames = received.shape[0]
    width, row_count = normed.shape
    locations = row_count // frames

    def unpack(b, carry):
        rows = pl.ds(pl.multiple_of(b * locations, 16), locations)
        for j in range(width // LANES):
            by_frame[rows, LANES * j : LANES * (j + 1)] = received[b, 16 * j : 16 * j + 16, :]
        return carry

    lax.fori_loop(0, frames, unpack, 0)
    row = lax.broadcasted_iota(jnp.int32, (row_count, row_count), 0)
    column = lax.broadcasted_iota(jnp.int32, (row_count, row_count), 1)
    moved = (row == (column % frames) * locations + column // frames).astype(F32).astype(BF16)
    by_slot[...] = dot_over(by_frame[...], moved, 0, 0).astype(BF16)
    for start in range(0, row_count, LANES):
        chunk = slice(start, start + LANES)
        values_in = layer_norm(by_slot[:, chunk].astype(F32), 0)
        normed[:, chunk] = (values_in * (1.0 + levels[:, 4:5]) + levels[:, 3:4]).astype(BF16)
    arriving[0].wait()
    project(columns, normed, projected)
    attend(projected, attended, gains, 2, None, allowed, head_size)
    arriving[1].wait()
    projected[0:width, :] = jnp.dot(out_rows[...], attended[...], preferred_element_type=F32)
    for start in range(0, row_count, LANES):
        chunk = slice(start, start + LANES)
        updated = by_slot[:, chunk].astype(F32) + levels[:, 5:6] * projected[0:width, chunk]
        normed[:, chunk] = layer_norm(updated, 0).astype(BF16)
    predicted[...] = jnp.dot(w_final[...], normed[...], preferred_element_type=F32)


def projection_scratch(rows, width):
    return [
        pltpu.VMEM((3 * width, width), BF16),
        pltpu.VMEM((width, rows), BF16),
        pltpu.VMEM((3 * width, rows), F32),
    ]


def body(
    tokens,
    modulation,
    w_qkv_s,
    w_out_s,
    w_qkv_t,
    w_out_t,
    w_final,
    norm_gains,
    clip_tokens,
    block_clip,
):
    rows, width = tokens.shape[1:]
    head_size = norm_gains.shape[1]
    frames = block_clip.shape[0]
    seq = lax.axis_size("seq")
    locations = rows // seq
    position = lax.axis_index("seq")
    branch_index = lax.axis_index("cfg")
    levels = modulation.transpose(1, 0, 2)
    member = block_clip[:, None] == jnp.arange(clip_tokens.shape[0], dtype=jnp.int32)[None, :]
    lengths = jnp.sum(jnp.where(member, clip_tokens[None, :], 0), axis=1)
    gains = norm_gains.T
    slot_of = jnp.arange(TEMPORAL_ROWS, dtype=jnp.int32) // frames
    clip_of = jnp.tile(block_clip, TEMPORAL_ROWS // frames)
    allowed = ((slot_of[:, None] == slot_of[None, :]) & (clip_of[:, None] == clip_of[None, :])).astype(F32)

    first_rows = jnp.pad(w_qkv_s.T, ((0, -w_qkv_s.shape[1] % 8), (0, 0)))
    later_rows = jnp.concatenate([w_qkv_t.T, w_out_t.T, w_out_s.T], axis=0)
    later_rows = jnp.pad(later_rows, ((0, -later_rows.shape[0] % 32), (0, 0)))
    gathered = lax.all_gather(later_rows, ("seq", "cfg"), axis=0, tiled=False)
    shards = gathered.shape[0]
    row_parts, ring_parts = spread_in_plane(first_rows, branch_index)
    small = pltpu.CompilerParams(vmem_limit_bytes=40 * 2**20)
    params = pltpu.CompilerParams(vmem_limit_bytes=58 * 2**20)
    vmem = pl.BlockSpec(memory_space=pltpu.VMEM)
    smem = pl.BlockSpec(memory_space=pltpu.SMEM)
    anywhere = pl.BlockSpec(memory_space=pl.ANY)
    tile_rows = locations * width // LANES
    cost = pl.CostEstimate(flops=20_000_000_000, bytes_accessed=20_000_000, transcendentals=0)
    attended = pl.pallas_call(
        functools.partial(spatial_kernel, head_size),
        out_shape=jax.ShapeDtypeStruct((width, rows), BF16),
        in_specs=[smem, smem, vmem, vmem, vmem] + [anywhere] * 14,
        out_specs=vmem,
        scratch_shapes=[pltpu.VMEM((shards,) + first_rows.shape, BF16)]
        + projection_scratch(rows, width)
        + [pltpu.SemaphoreType.DMA],
        compiler_params=small,
        cost_estimate=cost,
        name="spatial",
    )(clip_tokens, block_clip, tokens[0], levels, gains, *row_parts, *ring_parts)
    residual = pl.pallas_call(
        functools.partial(mixing_kernel, head_size),
        out_shape=jax.ShapeDtypeStruct((seq, tile_rows, LANES), BF16),
        in_specs=[vmem, vmem, vmem, anywhere],
        out_specs=vmem,
        scratch_shapes=[
            pltpu.VMEM((shards, 32, width), BF16),
            pltpu.VMEM((width, width), BF16),
            pltpu.SemaphoreType.DMA,
        ],
        compiler_params=params,
        cost_estimate=cost,
        name="mixing",
    )(tokens[0], levels, attended, gathered)
    received = lax.all_to_all(residual, "seq", split_axis=0, concat_axis=0, tiled=True)
    held = pl.pallas_call(
        functools.partial(prepare_kernel, head_size),
        out_shape=[
            jax.ShapeDtypeStruct((3 * width, width), BF16),
            jax.ShapeDtypeStruct((width, width), BF16),
        ],
        in_specs=[anywhere],
        out_specs=[vmem] * 2,
        scratch_shapes=[pltpu.VMEM((shards, 80, width), BF16), pltpu.SemaphoreType.DMA],
        compiler_params=params,
        cost_estimate=pl.CostEstimate(flops=0, bytes_accessed=30_000_000, transcendentals=0),
        name="prepare",
    )(gathered)
    predicted = pl.pallas_call(
        functools.partial(temporal_kernel, head_size),
        out_shape=jax.ShapeDtypeStruct((w_final.shape[1], rows), F32),
        in_specs=[vmem] * 5 + [anywhere] * 2,
        out_specs=vmem,
        scratch_shapes=projection_scratch(rows, width)
        + [
            pltpu.VMEM((width, width), BF16),
            pltpu.VMEM((width, rows), BF16),
            pltpu.VMEM((rows, width), BF16),
            pltpu.VMEM((width, rows), BF16),
            pltpu.SemaphoreType.DMA((2,)),
        ],
        compiler_params=params,
        cost_estimate=cost,
        name="temporal",
    )(received, modulation[0].T, gains, allowed, w_final.T, *held)

    half = predicted.shape[0] // 2
    outgoing = lax.dynamic_slice_in_dim(predicted, (1 - branch_index) * half, half, 0)
    other = lax.ppermute(outgoing, "cfg", [(0, 1), (1, 0)])
    own_part = lax.dynamic_slice_in_dim(predicted, branch_index * half, half, 0)
    conditional = jnp.where(branch_index == 0, own_part, other)
    unconditional = jnp.where(branch_index == 0, other, own_part)
    guided = (unconditional + 7.0 * (conditional - unconditional)).reshape(half, locations, frames)
    location_ids = position * locations + jnp.arange(locations, dtype=jnp.int32)
    inside = location_ids[:, None] < lengths[None, :]
    return jnp.where(inside[None], guided, 0.0).transpose(2, 1, 0)


def solution(mesh):
    in_specs = (
        P(("rep", "seq"), None, None),
        P("cfg", None, None),
        P(None, ("seq", "cfg")),
        P(None, ("seq", "cfg")),
        P(None, ("seq", "cfg")),
        P(None, ("seq", "cfg")),
        P(),
        P(),
        P("rep"),
        P("rep"),
    )
    out_specs = P("rep", "seq", "cfg")
    return jax.shard_map(body, mesh=mesh, in_specs=in_specs, out_specs=out_specs, check_vma=False)
```

```python
import functools
import math

import jax
import jax.numpy as jnp
from jax import lax
from jax.experimental import pallas as pl
from jax.experimental.pallas import tpu as pltpu
from jax.sharding import PartitionSpec as P

BF16 = jnp.bfloat16
F32 = jnp.float32
LANES = 128
TEMPORAL_ROWS = 256
X_RING, Z_RING, SPLIT = 4, 8, 512
X_SLOTS = (0, -1, 1, 2)
Z_SLOTS = (0, -1, -2, -3, 1, 2, 3, 4)

def swap_cores(array):
    return lax.ppermute(array, "cfg", [(0, 1), (1, 0)])


def plane_step(array, along_x, far=1):
    pairs = []
    for x in range(X_RING):
        for z in range(Z_RING):
            for core in range(2):
                by = (1 - 2 * core) * far
                to = ((x + by) % X_RING, z) if along_x else (x, (z + by) % Z_RING)
                pairs.append((2 * (x * Z_RING + z) + core, 2 * (to[0] * Z_RING + to[1]) + core))
    return lax.ppermute(array, ("seq", "cfg"), pairs)


def in_core_order(core, first, second):
    return jnp.where(core == 0, first, second), jnp.where(core == 0, second, first)


def spread_in_plane(own, core):
    pair = jnp.stack(in_core_order(core, own, swap_cores(own)))
    first, second = pair[:, :, :SPLIT], pair[:, :, SPLIT:]

    def own_half(parts):
        return lax.dynamic_index_in_dim(parts, core, 0, keepdims=True)

    near = [plane_step(second, False, far) for far in (1, 2, 3)]
    near.append(plane_step(own_half(second), False, 4))
    mine = jnp.concatenate([plane_step(first, True), plane_step(own_half(first), True, 2)])
    theirs = swap_cores(mine)
    low, high = in_core_order(core, mine[:2], theirs[:2])
    opposite = jnp.concatenate(in_core_order(core, mine[2:], theirs[2:]))
    row = jnp.stack([first, low, high, opposite])
    rows = [row]
    for _ in range(3):
        rows.append(plane_step(rows[-1], False))
    mine = jnp.concatenate(near)
    theirs = swap_cores(mine)
    low, high = in_core_order(core, mine[:6], theirs[:6])
    opposite = jnp.concatenate(in_core_order(core, mine[6:], theirs[6:]))
    ring = jnp.concatenate([second, low, high, opposite]).reshape((Z_RING,) + second.shape)
    across = plane_step(ring, True)
    beyond = plane_step(lax.dynamic_slice_in_dim(across, 4 * core, 4, 0), True)
    rows.append(plane_step(lax.dynamic_slice_in_dim(rows[3], 2 * core, 2, 0), False))
    rows += [swap_cores(part) for part in rows[1:]]
    return rows, [ring, across, beyond, swap_cores(across), swap_cores(beyond)]


def pick(table, index):
    found = table[-1]
    for i in range(len(table) - 1):
        found = jnp.where(index == i, table[i], found)
    return found


def plane_copies(rows, rings, landing, sem):
    position, core = lax.axis_index("seq"), lax.axis_index("cfg")
    x, z = position // Z_RING, position % Z_RING
    sign = 1 - 2 * core
    rest = landing.shape[2] - SPLIT
    copies = []

    def to_landing(part, dx, dz, columns):
        shard = 2 * (lax.rem(x + dx + X_RING, X_RING) * Z_RING + lax.rem(z + dz + Z_RING, Z_RING))
        copies.append(pltpu.make_async_copy(part, landing.at[pl.ds(shard, 2), :, columns], sem))

    for k in range(9):
        hop = k if k < 5 else k - 4
        dz = -sign * hop if k < 5 else sign * hop
        for j in range(rows[k].shape[0]):
            dx = X_SLOTS[j] if hop < 4 else pick(X_SLOTS, (2 * core if k < 5 else 2 - 2 * core) + j)
            to_landing(rows[k].at[j], dx, dz, pl.ds(0, SPLIT))
    for part, dx, start in zip(rings, (0, -sign, 2, sign, 2), (0, 0, 4 * core, 0, 4 - 4 * core)):
        for j in range(part.shape[0]):
            dz = Z_SLOTS[j] if part.shape[0] == Z_RING else pick(Z_SLOTS, start + j)
            to_landing(part.at[j], dx, dz, pl.ds(SPLIT, rest))
    return copies


def dot_over(left, right, left_dim, right_dim):
    return lax.dot_general(
        left, right, (((left_dim,), (right_dim,)), ((), ())), preferred_element_type=F32
    )


def layer_norm(values_in, axis):
    average = jnp.mean(values_in, axis=axis, keepdims=True)
    centred = values_in - average
    variance = jnp.mean(centred * centred, axis=axis, keepdims=True)
    return centred * lax.rsqrt(variance + 1e-06)


def lay_out(landing, target, first, count, arriving=None):
    size = 8 * count

    def group(g, carry):
        if arriving is not None:
            arriving(g).wait()
        rows = [landing[8 * g + i][first : first + count] for i in range(8)]
        target[pl.ds(pl.multiple_of(g * size, 16), size), :] = jnp.concatenate(rows, axis=0)
        return carry

    lax.fori_loop(0, landing.shape[0] // 8, group, 0)


def project(columns, normed, projected):
    width = normed.shape[0]

    def kind(i, carry):
        rows = pl.ds(pl.multiple_of(i * width, 16), width)
        projected[rows, :] = jnp.dot(columns[rows, :], normed[...], preferred_element_type=F32)
        return carry

    lax.fori_loop(0, 3, kind, 0)


def unit_heads(head, gain_column):
    total = jnp.sum(head * head, axis=0, keepdims=True)
    return (head * lax.rsqrt(total / head.shape[0] + 1e-06) * gain_column).astype(BF16)


def attend(projected, attended, gains, first_gain, inside, allowed, head_size):
    width = attended.shape[0]
    row_count = attended.shape[1]
    block = row_count if allowed is None else allowed.shape[0]
    factor = math.log2(math.e) / math.sqrt(head_size)
    query_gain = gains[:, first_gain : first_gain + 1] * factor
    key_gain = gains[:, first_gain + 1 : first_gain + 2]
    ones = jnp.ones((1, row_count), F32)
    blank = jnp.zeros((7, row_count), F32)

    def head(h):
        def part(kind):
            return projected[pl.ds(pl.multiple_of(kind * width + h * head_size, 8), head_size), :]

        query = unit_heads(part(0), query_gain)
        key = unit_heads(part(1), key_gain)
        value = jnp.concatenate([part(2), ones, blank], axis=0)
        if inside is not None:
            value = jnp.where(inside, value, 0.0)
        value = value.astype(BF16)
        found = []
        for start in range(0, row_count, block):
            tokens = slice(start, start + block)
            unnormed = jnp.exp2(dot_over(key[:, tokens], query[:, tokens], 0, 0))
            if allowed is not None:
                unnormed = unnormed * allowed[...]
            summed = jnp.dot(value[:, tokens], unnormed.astype(BF16), preferred_element_type=F32)
            found.append(summed[:head_size] / summed[head_size : head_size + 1])
        return jnp.concatenate(found, axis=1) if len(found) > 1 else found[0]

    def pair(p, carry):
        both = jnp.concatenate([head(2 * p), head(2 * p + 1)], axis=0)
        rows = pl.ds(pl.multiple_of(2 * head_size * p, 16), 2 * head_size)
        attended[rows, :] = both.astype(BF16)
        return carry

    lax.fori_loop(0, width // (2 * head_size), pair, 0)


def spatial_kernel(head_size, clip_tokens, block_clip, tokens, levels, gains, *refs):
    rows, rings = refs[:9], refs[9:14]
    attended, landing, columns, normed, projected, sem = refs[14:]
    arriving = plane_copies(rows, rings, landing, sem)
    for copy in arriving:
        copy.start()
    row_count = tokens.shape[0]
    for start in range(0, row_count, LANES):
        chunk = slice(start, start + LANES)
        values_in = layer_norm(tokens[chunk, :].astype(F32), 1) * (1.0 + levels[1]) + levels[0]
        normed[:, chunk] = values_in.astype(BF16).T
    for copy in arriving:
        copy.wait()
    lay_out(landing, columns, 0, 3 * head_size // 4)
    project(columns, normed, projected)
    length = clip_tokens[block_clip[lax.axis_index("seq")]]
    inside = lax.broadcasted_iota(jnp.int32, (head_size + 8, row_count), 1) < length
    attend(projected, attended, gains, 0, inside, None, head_size)


def mixing_kernel(head_size, tokens, levels, attended, gathered, residual, landing, out_rows, sems):
    first, kept = landing.shape[1] * 2, landing.shape[1]

    def arriving(g):
        shards = pl.ds(8 * g, 8)
        return pltpu.make_async_copy(gathered.at[shards, pl.ds(first, kept), :], landing.at[shards], sems.at[g])

    for g in range(landing.shape[0] // 8):
        arriving(g).start()
    lay_out(landing, out_rows, head_size - first, head_size // 4, arriving)
    for start in range(0, tokens.shape[0], 256):
        chunk = slice(start, start + 256)
        projection = dot_over(attended[:, chunk], out_rows[...], 0, 1)
        updated = (tokens[chunk, :].astype(F32) + levels[2] * projection).astype(BF16)
        for d in range(16):
            for j in range(residual.shape[1] // 16):
                residual[start // 16 + d, 16 * j : 16 * j + 16, :] = updated[
                    16 * d : 16 * d + 16, LANES * j : LANES * (j + 1)
                ]


def prepare_kernel(head_size, gathered, columns, out_rows, landing, sem):
    arriving = pltpu.make_async_copy(gathered.at[:, pl.ds(0, landing.shape[1]), :], landing, sem)
    arriving.start()
    arriving.wait()
    share = 3 * head_size // 4
    lay_out(landing, columns, 0, share)
    lay_out(landing, out_rows, share, head_size // 4)


def temporal_kernel(head_size, received, levels, gains, allowed, w_final, held_columns, held_rows, predicted,
                    columns, normed, projected, out_rows, attended, by_frame, by_slot, sems):
    arriving = [
        pltpu.make_async_copy(held_columns, columns, sems.at[0]),
        pltpu.make_async_copy(held_rows, out_rows, sems.at[1]),
    ]
    for copy in arriving:
        copy.start()
    frames = received.shape[0]
    width, row_count = normed.shape
    locations = row_count // frames

    def unpack(b, carry):
        rows = pl.ds(pl.multiple_of(b * locations, 16), locations)
        for j in range(width // LANES):
            by_frame[rows, LANES * j : LANES * (j + 1)] = received[b, 16 * j : 16 * j + 16, :]
        return carry

    lax.fori_loop(0, frames, unpack, 0)
    row = lax.broadcasted_iota(jnp.int32, (row_count, row_count), 0)
    column = lax.broadcasted_iota(jnp.int32, (row_count, row_count), 1)
    moved = (row == (column % frames) * locations + column // frames).astype(F32).astype(BF16)
    by_slot[...] = dot_over(by_frame[...], moved, 0, 0).astype(BF16)
    for start in range(0, row_count, LANES):
        chunk = slice(start, start + LANES)
        values_in = layer_norm(by_slot[:, chunk].astype(F32), 0)
        normed[:, chunk] = (values_in * (1.0 + levels[:, 4:5]) + levels[:, 3:4]).astype(BF16)
    arriving[0].wait()
    project(columns, normed, projected)
    attend(projected, attended, gains, 2, None, allowed, head_size)
    arriving[1].wait()
    projected[0:width, :] = jnp.dot(out_rows[...], attended[...], preferred_element_type=F32)
    for start in range(0, row_count, LANES):
        chunk = slice(start, start + LANES)
        updated = by_slot[:, chunk].astype(F32) + levels[:, 5:6] * projected[0:width, chunk]
        normed[:, chunk] = layer_norm(updated, 0).astype(BF16)
    predicted[...] = jnp.dot(w_final[...], normed[...], preferred_element_type=F32)


def projection_scratch(rows, width):
    return [
        pltpu.VMEM((3 * width, width), BF16),
        pltpu.VMEM((width, rows), BF16),
        pltpu.VMEM((3 * width, rows), F32),
    ]


def body(
    tokens,
    modulation,
    w_qkv_s,
    w_out_s,
    w_qkv_t,
    w_out_t,
    w_final,
    norm_gains,
    clip_tokens,
    block_clip,
):
    rows, width = tokens.shape[1:]
    head_size = norm_gains.shape[1]
    frames = block_clip.shape[0]
    seq = lax.axis_size("seq")
    locations = rows // seq
    position = lax.axis_index("seq")
    branch_index = lax.axis_index("cfg")
    levels = modulation.transpose(1, 0, 2)
    member = block_clip[:, None] == jnp.arange(clip_tokens.shape[0], dtype=jnp.int32)[None, :]
    lengths = jnp.sum(jnp.where(member, clip_tokens[None, :], 0), axis=1)
    gains = norm_gains.T
    slot_of = jnp.arange(TEMPORAL_ROWS, dtype=jnp.int32) // frames
    clip_of = jnp.tile(block_clip, TEMPORAL_ROWS // frames)
    allowed = ((slot_of[:, None] == slot_of[None, :]) & (clip_of[:, None] == clip_of[None, :])).astype(F32)

    first_rows = jnp.pad(w_qkv_s.T, ((0, -w_qkv_s.shape[1] % 8), (0, 0)))
    later_rows = jnp.concatenate([w_qkv_t.T, w_out_t.T, w_out_s.T], axis=0)
    later_rows = jnp.pad(later_rows, ((0, -later_rows.shape[0] % 32), (0, 0)))
    gathered = lax.all_gather(later_rows, ("seq", "cfg"), axis=0, tiled=False)
    shards = gathered.shape[0]
    row_parts, ring_parts = spread_in_plane(first_rows, branch_index)
    small = pltpu.CompilerParams(vmem_limit_bytes=40 * 2**20)
    params = pltpu.CompilerParams(vmem_limit_bytes=58 * 2**20)
    vmem = pl.BlockSpec(memory_space=pltpu.VMEM)
    smem = pl.BlockSpec(memory_space=pltpu.SMEM)
    anywhere = pl.BlockSpec(memory_space=pl.ANY)
    tile_rows = locations * width // LANES
    cost = pl.CostEstimate(flops=20_000_000_000, bytes_accessed=20_000_000, transcendentals=0)
    attended = pl.pallas_call(
        functools.partial(spatial_kernel, head_size),
        out_shape=jax.ShapeDtypeStruct((width, rows), BF16),
        in_specs=[smem, smem, vmem, vmem, vmem] + [anywhere] * 14,
        out_specs=vmem,
        scratch_shapes=[pltpu.VMEM((shards,) + first_rows.shape, BF16)]
        + projection_scratch(rows, width)
        + [pltpu.SemaphoreType.DMA],
        compiler_params=small,
        cost_estimate=cost,
        name="spatial",
    )(clip_tokens, block_clip, tokens[0], levels, gains, *row_parts, *ring_parts)
    residual = pl.pallas_call(
        functools.partial(mixing_kernel, head_size),
        out_shape=jax.ShapeDtypeStruct((seq, tile_rows, LANES), BF16),
        in_specs=[vmem, vmem, vmem, anywhere],
        out_specs=vmem,
        scratch_shapes=[
            pltpu.VMEM((shards, 32, width), BF16),
            pltpu.VMEM((width, width), BF16),
            pltpu.SemaphoreType.DMA((shards // 8,)),
        ],
        compiler_params=params,
        cost_estimate=cost,
        name="mixing",
    )(tokens[0], levels, attended, gathered)
    received = lax.all_to_all(residual, "seq", split_axis=0, concat_axis=0, tiled=True)
    held = pl.pallas_call(
        functools.partial(prepare_kernel, head_size),
        out_shape=[
            jax.ShapeDtypeStruct((3 * width, width), BF16),
            jax.ShapeDtypeStruct((width, width), BF16),
        ],
        in_specs=[anywhere],
        out_specs=[vmem] * 2,
        scratch_shapes=[pltpu.VMEM((shards, 80, width), BF16), pltpu.SemaphoreType.DMA],
        compiler_params=params,
        cost_estimate=pl.CostEstimate(flops=0, bytes_accessed=30_000_000, transcendentals=0),
        name="prepare",
    )(gathered)
    predicted = pl.pallas_call(
        functools.partial(temporal_kernel, head_size),
        out_shape=jax.ShapeDtypeStruct((w_final.shape[1], rows), F32),
        in_specs=[vmem] * 5 + [anywhere] * 2,
        out_specs=vmem,
        scratch_shapes=projection_scratch(rows, width)
        + [
            pltpu.VMEM((width, width), BF16),
            pltpu.VMEM((width, rows), BF16),
            pltpu.VMEM((rows, width), BF16),
            pltpu.VMEM((width, rows), BF16),
            pltpu.SemaphoreType.DMA((2,)),
        ],
        compiler_params=params,
        cost_estimate=cost,
        name="temporal",
    )(received, modulation[0].T, gains, allowed, w_final.T, *held)

    half = predicted.shape[0] // 2
    outgoing = lax.dynamic_slice_in_dim(predicted, (1 - branch_index) * half, half, 0)
    other = lax.ppermute(outgoing, "cfg", [(0, 1), (1, 0)])
    own_part = lax.dynamic_slice_in_dim(predicted, branch_index * half, half, 0)
    conditional = jnp.where(branch_index == 0, own_part, other)
    unconditional = jnp.where(branch_index == 0, other, own_part)
    guided = (unconditional + 7.0 * (conditional - unconditional)).reshape(half, locations, frames)
    location_ids = position * locations + jnp.arange(locations, dtype=jnp.int32)
    inside = location_ids[:, None] < lengths[None, :]
    return jnp.where(inside[None], guided, 0.0).transpose(2, 1, 0)


def solution(mesh):
    in_specs = (
        P(("rep", "seq"), None, None),
        P("cfg", None, None),
        P(None, ("seq", "cfg")),
        P(None, ("seq", "cfg")),
        P(None, ("seq", "cfg")),
        P(None, ("seq", "cfg")),
        P(),
        P(),
        P("rep"),
        P("rep"),
    )
    out_specs = P("rep", "seq", "cfg")
    return jax.shard_map(body, mesh=mesh, in_specs=in_specs, out_specs=out_specs, check_vma=False)
```
